512 devices in a mesh: dp: 64 (over x, y, core), tensor: 8 (over z).
Axes of the slice: x: 4, y: 8, z: 8, core: 2. Of those that a mesh axis runs over, the one named last changes fastest.
Arguments:
- grad: bfloat16 [64, 1024, 6144], P('dp', 'tensor'), may hold values from -40 to 40
- error: bfloat16 [64, 1024, 6144], P('dp', 'tensor'), may hold values from -4 to 4
- q_in: bfloat16 [6144, 64], P('tensor'), may hold values from -6 to 6
Outputs:
- new_error: bfloat16 [64, 1024, 6144], P('dp', 'tensor')
- p_factor: float32 [1024, 64], P('tensor')
- q_next: bfloat16 [6144, 64], P('tensor')
The draws below stay inside these ranges and needn't reach their ends.
All inputs are finite; a program needn't handle non-finite values.
Results may differ from the reference program's by a relative error of at most 0.0045.
The reference program's roundings to bfloat16 on the way (of `merged` and `p_round`) count: a program that leaves them out, or rounds other values in their place, can miss the bound.
Values may be sent and summed in bfloat16 or wider, within the bound.
No kernel may reach another device: no remote copies, remote signals or barrier semaphores. Data moves between devices by JAX's collectives and lax.ppermute only.
A program may use at most 64 MiB of HBM per device.

```python
import jax
import jax.numpy as jnp
from jax import lax

D = 6144
RANK = 64
ROWS = 1024
REPLICAS = 64


def draw_grad(key, part):
    key = jax.random.fold_in(key, 11)
    key_base = jax.random.fold_in(key, 0)
    key_noise = jax.random.fold_in(key, 1)
    key_offset = jax.random.fold_in(key, 3)
    offset = jax.random.randint(key_offset, (), 0, REPLICAS)
    column_owner = (jnp.arange(D) * REPLICAS // D + offset) % REPLICAS
    replica_ids = jnp.arange(REPLICAS)
    boost = jnp.where(column_owner[None, :] == replica_ids[:, None], 12.0, 1.0).astype(jnp.float32)
    base = jnp.clip(jax.random.normal(key_base, (ROWS, D), jnp.float32), -5.0, 5.0)
    noise = jnp.clip(jax.random.normal(key_noise, (REPLICAS, ROWS, D), jnp.float32), -5.0, 5.0)
    noise = noise * boost[:, None, :]
    return (base[None] + 0.5 * noise).astype(jnp.bfloat16)


def shard_levels(rng, shape, pieces, least, high):
    factor_of, own = 1.0, jax.random.fold_in(rng, 6)
    for axis_at, shards_of in pieces:
        draws = jnp.exp(jax.random.uniform(jax.random.fold_in(own, axis_at), (shards_of,), jnp.float32, least / len(pieces), high / len(pieces)))
        factor_of = factor_of * jnp.repeat(draws, shape[axis_at] // shards_of).reshape([-1 if axis == axis_at else 1 for axis in range(len(shape))])
    return factor_of


def scatter_about(key, shape, spread, reach, shards=(), held_as=jnp.bfloat16):
    values = jax.random.normal(key, shape, jnp.float32) * spread
    if len(shards) > 0:
        values = shard_levels(key, shape, shards, -0.22, 0.18) * values
    return jnp.clip(values, min=-reach, max=reach).astype(held_as)


def setup_inputs(seed: int = 0) -> dict:
    keys = jax.random.split(jax.random.key(seed), 4)
    return {
        "grad": draw_grad(jax.random.fold_in(keys[3], 71), 0),
        "error": scatter_about(keys[1], (REPLICAS, ROWS, D), 0.5, 4.0, ((0, 64), (1, 8))),
        "q_in": scatter_about(keys[2], (D, RANK), 1.0, 6.0, ((0, 8),)),
    }


def merge_pair(grad_one, error_one):
    return (grad_one.astype(jnp.float32) + error_one.astype(jnp.float32)).astype(jnp.bfloat16)

def reference(grad, error, q_in):

    def left_step(carry, pair):
        merged = merge_pair(pair[0], pair[1])
        return (carry + jnp.dot(merged.astype(jnp.float32), q_in.astype(jnp.float32), preferred_element_type=jnp.float32), None)
    p_sum, _ = lax.scan(left_step, jnp.zeros((ROWS, RANK), jnp.float32), (grad, error))
    gram = jnp.dot(p_sum.T, p_sum, precision=lax.Precision.HIGHEST)
    chol = jnp.linalg.cholesky(gram)
    p_factor = lax.linalg.triangular_solve(chol, p_sum, left_side=False, lower=True, transpose_a=True)
    p_round = p_factor.astype(jnp.bfloat16)

    def right_step(carry, pair):
        merged = merge_pair(pair[0], pair[1])
        term = lax.dot_general(merged.astype(jnp.float32), p_round.astype(jnp.float32), (((0,), (0,)), ((), ())), preferred_element_type=jnp.float32)
        return (carry + term, None)
    q_sum, _ = lax.scan(right_step, jnp.zeros((D, RANK), jnp.float32), (grad, error))
    q_next = (q_sum / REPLICAS).astype(jnp.bfloat16)
    decoded = jnp.dot(p_round.astype(jnp.float32), q_next.T.astype(jnp.float32), preferred_element_type=jnp.float32)

    def error_step(pair):
        return (pair[0].astype(jnp.float32) + pair[1].astype(jnp.float32) - decoded).astype(jnp.bfloat16)
    new_error = lax.map(error_step, (grad, error))
    return (new_error, p_factor, q_next)
```

```python
import functools

import jax
import jax.numpy as jnp
from jax import lax
from jax.experimental import pallas as pl
from jax.experimental.pallas import tpu as pltpu
from jax.sharding import Mesh, PartitionSpec as P

F32, BF16 = jnp.float32, jnp.bfloat16
SMEM = pl.BlockSpec(memory_space=pltpu.SMEM)
VMEM = pl.BlockSpec(memory_space=pltpu.VMEM)
PLANE = ("x", "y")
REPLICA = ("x", "y", "core")


def merge_kernel(core_ref, grad_ref, error_ref, keep_ref, give_ref):
    half = keep_ref.shape[-1]
    merged = (grad_ref[...].astype(F32) + error_ref[...].astype(F32)).astype(BF16)
    low, high = merged[:, :half], merged[:, half:]

    @pl.when(core_ref[0] == 0)
    def _():
        keep_ref[0], give_ref[0] = low, high

    @pl.when(core_ref[0] != 0)
    def _():
        keep_ref[0], give_ref[0] = high, low


def left_kernel(factor_ref, keep_ref, took_ref, out_ref):
    @pl.when(pl.program_id(0) == 0)
    def _():
        out_ref[...] = jnp.zeros_like(out_ref)

    lanes = (((1,), (1,)), ((), ()))
    out_ref[...] += lax.dot_general(
        factor_ref[0], keep_ref[0], lanes, preferred_element_type=F32
    ) + lax.dot_general(
        factor_ref[0], took_ref[0], lanes, preferred_element_type=F32
    )


def gram_kernel(left_ref, out_ref):
    left = left_ref[...]
    out_ref[...] = lax.dot_general(
        left, left, (((1,), (1,)), ((), ())),
        precision=lax.Precision.HIGHEST, preferred_element_type=F32,
    )


def factor_kernel(grams_ref, left_ref, factor_ref, round_ref):
    gram = grams_ref[0]
    for part in range(1, grams_ref.shape[0]):
        gram = gram + grams_ref[part]
    rank = gram.shape[0]
    blocks = rank // 8
    rows = [
        (gram[8 * b : 8 * b + 8], left_ref[8 * b : 8 * b + 8, :]) for b in range(blocks)
    ]
    sub = lax.broadcasted_iota(jnp.int32, (8, 1), 0)
    for k in range(rank):
        own, at = k // 8, k % 8
        gram_row = rows[own][0][at : at + 1, :]
        left_row = rows[own][1][at : at + 1, :]
        inverse = 1.0 / gram_row[:, k : k + 1]
        gram_row, left_row = gram_row * inverse, left_row * inverse
        for b in range(own, blocks):
            column = rows[b][0][:, k : k + 1]
            if b == own:
                column = jnp.where(sub > at, column, 0.0)
            rows[b] = (rows[b][0] - column * gram_row, rows[b][1] - column * left_row)
    lane = lax.broadcasted_iota(jnp.int32, (8, rank), 1)
    for b in range(blocks):
        row = lax.broadcasted_iota(jnp.int32, (8, rank), 0) + 8 * b
        pivot = jnp.sum(jnp.where(lane == row, rows[b][0], 0.0), axis=1, keepdims=True)
        factor_ref[8 * b : 8 * b + 8, :] = rows[b][1] / jnp.sqrt(pivot)
    round_ref[...] = factor_ref[...].astype(BF16)


def right_kernel(round_ref, keep_ref, took_ref, out_ref):
    out_ref[0] = jnp.dot(
        round_ref[...], keep_ref[0], preferred_element_type=F32
    ) + jnp.dot(round_ref[...], took_ref[0], preferred_element_type=F32)


def decode_kernel(core_ref, round_ref, own_ref, other_ref, grad_ref, error_ref, out_ref):
    half = own_ref.shape[-1]
    first = core_ref[0] == 0
    own, other = own_ref[0], other_ref[0]
    for part in range(2):
        factor = jnp.where(first if part == 0 else jnp.logical_not(first), own, other)
        decoded = lax.dot_general(
            round_ref[...], factor, (((0,), (0,)), ((), ())), preferred_element_type=F32
        )
        at = pl.ds(part * half, half)
        out_ref[:, at] = (
            grad_ref[:, at].astype(F32) + error_ref[:, at].astype(F32) - decoded
        ).astype(BF16)


def spread(block, axes, count):
    return lax.all_to_all(jnp.broadcast_to(block[None], (count, *block.shape)), axes, 0, 0)


def local(sizes, grad, error, q_in):
    planes, shards, cores = sizes["x"] * sizes["y"], sizes["z"], sizes["core"]
    replicas = planes * cores
    grad, error = grad[0], error[0]
    height, width = grad.shape
    cols, rank = q_in.shape
    half = cols // cores
    core = lax.axis_index("core")
    core_id = core.reshape(1)
    swap = [(0, 1), (1, 0)]

    whole = pl.BlockSpec((height, cols), lambda i: (0, i))
    piece = pl.BlockSpec((1, height, half), lambda i: (i, 0, 0))
    factors = pl.BlockSpec((1, rank, half), lambda i: (i, 0, 0))
    small = pl.BlockSpec((rank, height), lambda i: (0, 0))

    keep, give = pl.pallas_call(
        merge_kernel,
        grid=(shards,),
        in_specs=[SMEM, whole, whole],
        out_specs=[piece, piece],
        out_shape=[jax.ShapeDtypeStruct((shards, height, half), BF16)] * 2,
        name="merge",
    )(core_id, grad, error)
    took = lax.ppermute(give, "core", swap)

    q_mine = lax.dynamic_slice_in_dim(q_in.T, core * half, half, 1)
    q_all = spread(q_mine, "z", shards)
    left = pl.pallas_call(
        left_kernel,
        grid=(shards,),
        in_specs=[factors, piece, piece],
        out_specs=small,
        out_shape=jax.ShapeDtypeStruct((rank, height), F32),
        name="left",
    )(q_all, keep, took)
    left_row = lax.all_to_all(left.reshape(replicas, -1, height), REPLICA, 0, 0).sum(0)
    left_sum = spread(left_row, REPLICA, replicas).reshape(rank, height)

    gram = pl.pallas_call(
        gram_kernel,
        in_specs=[VMEM],
        out_specs=VMEM,
        out_shape=jax.ShapeDtypeStruct((rank, rank), F32),
        name="gram",
    )(left_sum)
    grams = spread(gram, "z", shards)
    p_factor, p_round = pl.pallas_call(
        factor_kernel,
        in_specs=[VMEM, VMEM],
        out_specs=[VMEM, VMEM],
        out_shape=[
            jax.ShapeDtypeStruct((rank, height), F32),
            jax.ShapeDtypeStruct((rank, height), BF16),
        ],
        name="factor",
    )(grams, left_sum)

    right = pl.pallas_call(
        right_kernel,
        grid=(shards,),
        in_specs=[small, piece, piece],
        out_specs=factors,
        out_shape=jax.ShapeDtypeStruct((shards, rank, half), F32),
        name="right",
    )(p_round, keep, took)
    right = lax.all_to_all(right, "z", 0, 0).sum(0)
    right = lax.all_to_all(right.reshape(planes, -1, half), PLANE, 0, 0).sum(0)
    q_rows = (right / replicas).astype(BF16)
    q_block = spread(q_rows, PLANE, planes).reshape(rank, half)
    q_own = spread(q_block, "z", shards)
    q_other = lax.ppermute(q_own, "core", swap)

    new_error = pl.pallas_call(
        decode_kernel,
        grid=(shards,),
        in_specs=[SMEM, small, factors, factors, whole, whole],
        out_specs=whole,
        out_shape=jax.ShapeDtypeStruct((height, cols * shards), BF16),
        name="decode",
    )(core_id, p_round, q_own, q_other, grad, error)

    z = lax.axis_index("z")
    q_pair = [
        lax.dynamic_index_in_dim(q, z, 0, keepdims=False) for q in (q_own, q_other)
    ]
    first = core == 0
    q_next = jnp.concatenate(
        [
            jnp.where(first, q_pair[0], q_pair[1]),
            jnp.where(first, q_pair[1], q_pair[0]),
        ],
        axis=1,
    )
    return new_error[None], p_factor.T, q_next.T


def solution(mesh):
    sizes = {"x": 4, "y": 8, "core": 2, "z": 8}
    fine = Mesh(mesh.devices.reshape(tuple(sizes.values())), tuple(sizes))
    placed = (P(REPLICA, "z", None), P(REPLICA, "z", None), P("z", None))
    return jax.shard_map(
        functools.partial(local, sizes),
        mesh=fine,
        in_specs=placed,
        out_specs=(P(REPLICA, "z", None), P("z", None), P("z", None)),
        check_vma=False,
    )
```

```python
import functools

import jax
import jax.numpy as jnp
from jax import lax
from jax.experimental import pallas as pl
from jax.experimental.pallas import tpu as pltpu
from jax.sharding import Mesh, PartitionSpec as P

F32, BF16 = jnp.float32, jnp.bfloat16
SMEM = pl.BlockSpec(memory_space=pltpu.SMEM)
VMEM = pl.BlockSpec(memory_space=pltpu.VMEM)
ANY = pl.BlockSpec(memory_space=pl.ANY)
PLANE = ("x", "y")
REPLICA = ("x", "y", "core")
LIMIT = 32 * 2**20


def merge_kernel(core_ref, grad_hbm, error_hbm, keep_ref, give_ref, grad, error, sems):
    parts, _, half = keep_ref.shape
    cols = 2 * half
    copies = []
    for i in range(parts):
        at = pl.ds(i * cols, cols)
        copies.append(
            [
                pltpu.make_async_copy(src.at[:, at], dst.at[:, at], sems.at[j, i])
                for j, (src, dst) in enumerate(((grad_hbm, grad), (error_hbm, error)))
            ]
        )
        for copy in copies[-1]:
            copy.start()
    core = core_ref[0]
    for i in range(parts):
        for copy in copies[i]:
            copy.wait()
        for out, which in ((give_ref, 1 - core), (keep_ref, core)):
            at = pl.ds(pl.multiple_of(i * cols + which * half, half), half)
            out[i] = (grad[:, at].astype(F32) + error[:, at].astype(F32)).astype(BF16)


def left_kernel(factor_ref, keep_ref, took_ref, out_ref):
    height = keep_ref.shape[1]
    total = None
    for i in range(keep_ref.shape[0]):
        both = jnp.concatenate([keep_ref[i], took_ref[i]], axis=0)
        term = lax.dot_general(
            factor_ref[i], both, (((1,), (1,)), ((), ())), preferred_element_type=F32
        )
        total = term if total is None else total + term
    out_ref[...] = total[:, :height] + total[:, height:]


def gram_kernel(left_ref, out_ref):
    left = left_ref[...]
    gram = lax.dot_general(
        left, left, (((1,), (1,)), ((), ())),
        precision=lax.Precision.HIGHEST, preferred_element_type=F32,
    )
    packed = jnp.concatenate(jnp.split(gram, 2, axis=0), axis=1)
    for i in range(out_ref.shape[0]):
        out_ref[i] = packed


def factor_kernel(grams_ref, left_ref, factor_ref, round_ref):
    packed = grams_ref[0]
    for part in range(1, grams_ref.shape[0]):
        packed = packed + grams_ref[part]
    rank = packed.shape[1] // 2
    gram = jnp.concatenate([packed[:, :rank], packed[:, rank:]], axis=0)
    blocks = rank // 8
    rows = [
        (gram[8 * b : 8 * b + 8], left_ref[8 * b : 8 * b + 8, :]) for b in range(blocks)
    ]
    sub = lax.broadcasted_iota(jnp.int32, (8, 1), 0)
    for k in range(0, rank, 2):
        own, at = k // 8, k % 8
        g0, g1 = (rows[own][0][at + j : at + j + 1, :] for j in range(2))
        p0, p1 = (rows[own][1][at + j : at + j + 1, :] for j in range(2))
        a, b, d = g0[:, k : k + 1], g0[:, k + 1 : k + 2], g1[:, k + 1 : k + 2]
        det = a * d - b * b
        inverse = 1.0 / det
        factor_ref[k : k + 1, :] = p0 / jnp.sqrt(a)
        factor_ref[k + 1 : k + 2, :] = (p1 - (b / a) * p0) / jnp.sqrt(det / a)
        ai, bi, di = a * inverse, b * inverse, d * inverse
        u0, u1 = di * g0 - bi * g1, ai * g1 - bi * g0
        v0, v1 = di * p0 - bi * p1, ai * p1 - bi * p0
        for n in range(own, blocks):
            c0, c1 = rows[n][0][:, k : k + 1], rows[n][0][:, k + 1 : k + 2]
            if n == own:
                c0, c1 = (jnp.where(sub > at + 1, c, 0.0) for c in (c0, c1))
            rows[n] = (
                rows[n][0] - c0 * u0 - c1 * u1,
                rows[n][1] - c0 * v0 - c1 * v1,
            )
    round_ref[...] = factor_ref[...].astype(BF16)


def right_kernel(round_ref, keep_ref, took_ref, out_ref):
    twice = jnp.concatenate([round_ref[...], round_ref[...]], axis=1)
    for i in range(keep_ref.shape[0]):
        both = jnp.concatenate([keep_ref[i], took_ref[i]], axis=0)
        out_ref[i] = jnp.dot(twice, both, preferred_element_type=F32)


def decode_kernel(core_ref, round_ref, own_ref, other_ref, grad_hbm, error_hbm, out_hbm, grad, error, out, sems):
    parts, _, half = own_ref.shape
    cols = 2 * half
    copies = []
    for i in range(parts):
        at = pl.ds(i * cols, cols)
        copies.append(
            [
                pltpu.make_async_copy(src.at[:, at], dst.at[:, at], sems.at[j, i])
                for j, (src, dst) in enumerate(((grad_hbm, grad), (error_hbm, error)))
            ]
        )
        for copy in copies[-1]:
            copy.start()
    core = core_ref[0]
    rounded = round_ref[...]
    sent = []
    for i in range(parts):
        for copy in copies[i]:
            copy.wait()
        for factor_ref, which in ((own_ref, core), (other_ref, 1 - core)):
            decoded = lax.dot_general(
                rounded, factor_ref[i], (((0,), (0,)), ((), ())),
                preferred_element_type=F32,
            )
            at = pl.ds(pl.multiple_of(i * cols + which * half, half), half)
            out[:, at] = (
                grad[:, at].astype(F32) + error[:, at].astype(F32) - decoded
            ).astype(BF16)
        at = pl.ds(i * cols, cols)
        sent.append(pltpu.make_async_copy(out.at[:, at], out_hbm.at[:, at], sems.at[2, i]))
        sent[-1].start()
    for copy in sent:
        copy.wait()


def spread(block, axes, count):
    return lax.all_to_all(jnp.broadcast_to(block[None], (count, *block.shape)), axes, 0, 0)


def local(sizes, grad, error, q_in):
    planes, shards, cores = sizes["x"] * sizes["y"], sizes["z"], sizes["core"]
    replicas = planes * cores
    grad, error = grad[0], error[0]
    height, width = grad.shape
    cols, rank = q_in.shape
    half = cols // cores
    core = lax.axis_index("core")
    core_id = core.reshape(1)
    swap = [(0, 1), (1, 0)]

    pieces = jax.ShapeDtypeStruct((shards, height, half), BF16)
    staged = pltpu.VMEM((height, width), BF16)

    keep, give = pl.pallas_call(
        merge_kernel,
        in_specs=[SMEM, ANY, ANY],
        out_specs=[VMEM, VMEM],
        out_shape=[pieces, pieces],
        scratch_shapes=[staged, staged, pltpu.SemaphoreType.DMA((2, shards))],
        compiler_params=pltpu.CompilerParams(vmem_limit_bytes=LIMIT),
        name="merge",
    )(core_id, grad, error)
    took = lax.ppermute(give, "core", swap)

    q_mine = lax.dynamic_slice_in_dim(q_in.T, core * half, half, 1)
    q_all = spread(q_mine, "z", shards)
    left = pl.pallas_call(
        left_kernel,
        in_specs=[VMEM, VMEM, VMEM],
        out_specs=VMEM,
        out_shape=jax.ShapeDtypeStruct((rank, height), F32),
        compiler_params=pltpu.CompilerParams(vmem_limit_bytes=LIMIT),
        name="left",
    )(q_all, keep, took)
    left_row = lax.all_to_all(left.reshape(replicas, -1, height), REPLICA, 0, 0).sum(0)
    left_sum = spread(left_row, REPLICA, replicas).reshape(rank, height)

    gram = pl.pallas_call(
        gram_kernel,
        in_specs=[VMEM],
        out_specs=VMEM,
        out_shape=jax.ShapeDtypeStruct((shards, rank // 2, 2 * rank), F32),
        name="gram",
    )(left_sum)
    grams = lax.all_to_all(gram, "z", 0, 0)
    p_factor, p_round = pl.pallas_call(
        factor_kernel,
        in_specs=[VMEM, VMEM],
        out_specs=[VMEM, VMEM],
        out_shape=[
            jax.ShapeDtypeStruct((rank, height), F32),
            jax.ShapeDtypeStruct((rank, height), BF16),
        ],
        name="factor",
    )(grams, left_sum)

    right = pl.pallas_call(
        right_kernel,
        in_specs=[VMEM, VMEM, VMEM],
        out_specs=VMEM,
        out_shape=jax.ShapeDtypeStruct((shards, rank, half), F32),
        compiler_params=pltpu.CompilerParams(vmem_limit_bytes=LIMIT),
        name="right",
    )(p_round, keep, took)
    right = lax.all_to_all(right, "z", 0, 0).sum(0)
    right = lax.all_to_all(right.reshape(planes, -1, half), PLANE, 0, 0).sum(0)
    q_rows = (right / replicas).astype(BF16)
    q_block = spread(q_rows, PLANE, planes).reshape(rank, half)
    q_own = spread(q_block, "z", shards)
    q_other = lax.ppermute(q_own, "core", swap)

    new_error = pl.pallas_call(
        decode_kernel,
        in_specs=[SMEM, VMEM, VMEM, VMEM, ANY, ANY],
        out_specs=ANY,
        out_shape=jax.ShapeDtypeStruct((height, width), BF16),
        scratch_shapes=[staged] * 3 + [pltpu.SemaphoreType.DMA((3, shards))],
        compiler_params=pltpu.CompilerParams(vmem_limit_bytes=LIMIT),
        name="decode",
    )(core_id, p_round, q_own, q_other, grad, error)

    z = lax.axis_index("z")
    q_pair = [
        lax.dynamic_index_in_dim(q, z, 0, keepdims=False) for q in (q_own, q_other)
    ]
    first = core == 0
    q_next = jnp.concatenate(
        [
            jnp.where(first, q_pair[0], q_pair[1]),
            jnp.where(first, q_pair[1], q_pair[0]),
        ],
        axis=1,
    )
    return new_error[None], p_factor.T, q_next.T


def solution(mesh):
    sizes = {"x": 4, "y": 8, "core": 2, "z": 8}
    fine = Mesh(mesh.devices.reshape(tuple(sizes.values())), tuple(sizes))
    placed = (P(REPLICA, "z", None), P(REPLICA, "z", None), P("z", None))
    return jax.shard_map(
        functools.partial(local, sizes),
        mesh=fine,
        in_specs=placed,
        out_specs=(P(REPLICA, "z", None), P("z", None), P("z", None)),
        check_vma=False,
    )
```

```python
import functools

import jax
import jax.numpy as jnp
from jax import lax
from jax.experimental import pallas as pl
from jax.experimental.pallas import tpu as pltpu
from jax.sharding import Mesh, PartitionSpec as P

F32, BF16 = jnp.float32, jnp.bfloat16
SMEM = pl.BlockSpec(memory_space=pltpu.SMEM)
VMEM = pl.BlockSpec(memory_space=pltpu.VMEM)
HBM = pl.BlockSpec(memory_space=pltpu.HBM)
PLANE = ("x", "y")
REPLICA = ("x", "y", "core")
LIMIT = 16 * 2**20


def merge_kernel(core_ref, grad_hbm, error_hbm, keep_ref, give_ref, grad, error, sems):
    parts, _, half = keep_ref.shape
    cols = 2 * half
    copies = []
    for i in range(parts):
        at = pl.ds(i * cols, cols)
        copies.append(
            [
                pltpu.make_async_copy(src.at[:, at], dst.at[:, at], sems.at[j, i])
                for j, (src, dst) in enumerate(((grad_hbm, grad), (error_hbm, error)))
            ]
        )
        for copy in copies[-1]:
            copy.start()
    core = core_ref[0]
    for i in range(parts):
        for copy in copies[i]:
            copy.wait()
        for out, which in ((give_ref, 1 - core), (keep_ref, core)):
            at = pl.ds(pl.multiple_of(i * cols + which * half, half), half)
            out[i] = (grad[:, at].astype(F32) + error[:, at].astype(F32)).astype(BF16)


def pair_kernel(keep_ref, took_ref, out_ref):
    for i in range(out_ref.shape[0]):
        out_ref[i] = keep_ref[i].astype(F32) + took_ref[i].astype(F32)


def left_kernel(factor_ref, keep_ref, took_ref, out_ref):
    height = keep_ref.shape[1]
    total = None
    for i in range(keep_ref.shape[0]):
        both = jnp.concatenate([keep_ref[i], took_ref[i]], axis=0)
        term = lax.dot_general(
            factor_ref[i], both, (((1,), (1,)), ((), ())), preferred_element_type=F32
        )
        total = term if total is None else total + term
    out_ref[...] = total[:, :height] + total[:, height:]


def gram_kernel(left_ref, out_ref):
    left = left_ref[...]
    gram = lax.dot_general(
        left, left, (((1,), (1,)), ((), ())),
        precision=lax.Precision.HIGHEST, preferred_element_type=F32,
    )
    packed = jnp.concatenate(jnp.split(gram, 2, axis=0), axis=1)
    for i in range(out_ref.shape[0]):
        out_ref[i] = packed


def factor_kernel(grams_ref, left_ref, factor_ref, round_ref):
    packed = grams_ref[0]
    for part in range(1, grams_ref.shape[0]):
        packed = packed + grams_ref[part]
    rank = packed.shape[1] // 2
    gram = jnp.concatenate([packed[:, :rank], packed[:, rank:]], axis=0)
    gram = jnp.concatenate([gram, gram], axis=1)
    blocks = rank // 8
    g = [gram[8 * n : 8 * n + 8] for n in range(blocks)]
    p = [left_ref[8 * n : 8 * n + 8, :] for n in range(blocks)]
    full = (8, 2 * rank)
    sub = lax.broadcasted_iota(jnp.int32, full, 0)

    def lane(v, k):
        return jnp.broadcast_to(v[:, k : k + 1], full)

    def row(v, k):
        return jnp.broadcast_to(v[k : k + 1, :], full)

    hold = None
    for k in range(0, rank, 4):
        own, at = k // 8, k % 8
        gs = [row(g[own], at + j) for j in range(4)]
        ps = [row(p[own], at + j) for j in range(4)]
        e = {(i, j): lane(gs[i], k + j) for i in range(4) for j in range(i, 4)}
        a, b, d = e[0, 0], e[0, 1], e[1, 1]
        det = a * d - b * b
        inverse = 1.0 / det
        ai, bi, di = a * inverse, b * inverse, d * inverse
        t00, t01 = di * e[0, 2] - bi * e[1, 2], di * e[0, 3] - bi * e[1, 3]
        t10, t11 = ai * e[1, 2] - bi * e[0, 2], ai * e[1, 3] - bi * e[0, 3]
        a2 = e[2, 2] - e[0, 2] * t00 - e[1, 2] * t10
        b2 = e[2, 3] - e[0, 2] * t01 - e[1, 2] * t11
        d2 = e[3, 3] - e[0, 3] * t01 - e[1, 3] * t11
        det2 = a2 * d2 - b2 * b2
        inverse2 = 1.0 / det2
        ai2, bi2, di2 = a2 * inverse2, b2 * inverse2, d2 * inverse2

        def solve(r):
            s2 = r[2] - t00 * r[0] - t10 * r[1]
            s3 = r[3] - t01 * r[0] - t11 * r[1]
            w2, w3 = di2 * s2 - bi2 * s3, ai2 * s3 - bi2 * s2
            q0, q1 = di * r[0] - bi * r[1], ai * r[1] - bi * r[0]
            w0, w1 = q0 - t00 * w2 - t01 * w3, q1 - t10 * w2 - t11 * w3
            return (w0, w1, w2, w3), s2, s3

        u, _, _ = solve(gs)
        v, s2, s3 = solve(ps)
        done = (
            ps[0] / jnp.sqrt(a),
            (ps[1] - (b / a) * ps[0]) / jnp.sqrt(det / a),
            s2 / jnp.sqrt(a2),
            (s3 - (b2 / a2) * s2) / jnp.sqrt(det2 / a2),
        )
        out = done[0]
        for j in range(1, 4):
            out = jnp.where(sub == at + j, done[j], out)
        if at == 0:
            hold = out
        else:
            factor_ref[8 * own : 8 * own + 8, :] = jnp.where(sub < 4, hold, out)
        for n in range(own if at == 0 else own + 1, blocks):
            c = [lane(g[n], k + j) for j in range(4)]
            if n == own:
                c = [jnp.where(sub > at + 3, x, 0.0) for x in c]
            g[n] = g[n] - (c[0] * u[0] + c[1] * u[1]) - (c[2] * u[2] + c[3] * u[3])
            p[n] = p[n] - (c[0] * v[0] + c[1] * v[1]) - (c[2] * v[2] + c[3] * v[3])
    round_ref[...] = factor_ref[...].T.astype(BF16)


def right_kernel(slab_ref, round_ref, out_ref):
    slab = slab_ref[0]
    for i in range(1, slab_ref.shape[0]):
        slab = slab + slab_ref[i]
    term = jnp.dot(
        slab, round_ref[...].astype(F32),
        precision=lax.Precision.HIGHEST, preferred_element_type=F32,
    )
    packed = jnp.concatenate(jnp.split(term, 2, axis=0), axis=1)
    for i in range(out_ref.shape[0]):
        out_ref[i] = packed


def decode_kernel(place_ref, round_ref, own_ref, other_ref, grad, error, out_hbm, next_ref, out, sems):
    planes, fold, lanes = own_ref.shape
    rank = lanes // 2
    parts = grad.shape[1] // next_ref.shape[1]
    inner = planes // parts
    half = 2 * fold * inner
    cols = 2 * half
    core, z = place_ref[0], place_ref[1]
    rounded = round_ref[...]

    def factor(ref, part):
        pieces = []
        for x in range(inner):
            piece = ref[x * parts + part]
            pieces += [piece[:, :rank], piece[:, rank:]]
        return jnp.concatenate(pieces, axis=0)

    sent = []
    for i in range(parts):
        for ref, which in ((own_ref, core), (other_ref, 1 - core)):
            decoded = lax.dot_general(
                rounded, factor(ref, i), (((1,), (1,)), ((), ())),
                preferred_element_type=F32,
            )
            at = pl.ds(pl.multiple_of(i * cols + which * half, half), half)
            out[:, at] = (
                grad[:, at].astype(F32) + error[:, at].astype(F32) - decoded
            ).astype(BF16)
        at = pl.ds(i * cols, cols)
        sent.append(pltpu.make_async_copy(out.at[:, at], out_hbm.at[:, at], sems.at[i]))
        sent[-1].start()
    for ref, which in ((own_ref, core), (other_ref, 1 - core)):
        at = pl.ds(pl.multiple_of(which * half, half), half)
        next_ref[:, at] = factor(ref, z).astype(F32).T.astype(BF16)
    for copy in sent:
        copy.wait()


def call(kernel, name, out_shape, in_specs, out_specs=VMEM, scratch_shapes=()):
    return pl.pallas_call(
        kernel,
        in_specs=in_specs,
        out_specs=out_specs,
        out_shape=out_shape,
        scratch_shapes=scratch_shapes,
        compiler_params=pltpu.CompilerParams(vmem_limit_bytes=LIMIT),
        name=name,
    )


def spread(block, axes, count):
    return lax.all_to_all(jnp.broadcast_to(block[None], (count, *block.shape)), axes, 0, 0)


def local(sizes, grad, error, q_in):
    across, along, shards, cores = sizes["x"], sizes["y"], sizes["z"], sizes["core"]
    planes = across * along
    replicas = planes * cores
    grad, error = grad[0], error[0]
    height, width = grad.shape
    cols, rank = q_in.shape
    half = cols // cores
    core, z = lax.axis_index("core"), lax.axis_index("z")
    swap = [(0, 1), (1, 0)]
    array = jax.ShapeDtypeStruct

    pieces = array((along, height, half), BF16)
    staged = pltpu.VMEM((height, width), BF16)
    keep, give = call(
        merge_kernel, "merge", [pieces, pieces], [SMEM, HBM, HBM], [VMEM, VMEM],
        [staged, staged, pltpu.SemaphoreType.DMA((2, along))],
    )(core.reshape(1), grad, error)
    took = lax.ppermute(give, "core", swap)
    pair = call(pair_kernel, "pair", array(pieces.shape, F32), [VMEM, VMEM])(keep, took)
    q_in, pair = lax.optimization_barrier((q_in, pair))
    slab = lax.psum_scatter(pair, "y", scatter_dimension=0, tiled=True)[0]

    q_mine = lax.dynamic_slice_in_dim(q_in.T, core * half, half, 1)
    q_all = spread(q_mine, "z", shards)
    left = call(left_kernel, "left", array((rank, height), F32), [VMEM] * 3)(
        q_all, keep, took
    )
    left_row = lax.all_to_all(left.reshape(replicas, -1, height), REPLICA, 0, 0).sum(0)
    left_sum = spread(left_row, REPLICA, replicas).reshape(rank, height)

    gram = call(gram_kernel, "gram", array((shards, rank // 2, 2 * rank), F32), [VMEM])(
        left_sum
    )
    grams = lax.all_to_all(gram, "z", 0, 0)
    p_factor, p_round = call(
        factor_kernel, "factor",
        [array((rank, height), F32), array((height, rank), BF16)],
        [VMEM, VMEM], [VMEM, VMEM],
    )(grams, left_sum)

    fold = half // across
    slab = lax.all_to_all(slab.T.reshape(across, fold, height), "x", 0, 0)
    term = call(
        right_kernel, "right", array((shards, fold // 2, 2 * rank), F32), [VMEM, VMEM]
    )(slab, p_round)
    q_mine = (lax.all_to_all(term, "z", 0, 0).sum(0) / replicas).astype(BF16)
    q_own = spread(q_mine, PLANE, planes)
    q_other = lax.ppermute(q_own, "core", swap)

    new_error, q_next = call(
        decode_kernel, "decode",
        [array((height, width), BF16), array((rank, cols), BF16)],
        [SMEM] + [VMEM] * 5, [HBM, VMEM],
        [staged, pltpu.SemaphoreType.DMA((along,))],
    )(jnp.stack([core, z]), p_round, q_own, q_other, grad, error)
    return new_error[None], p_factor.T, q_next.T


def solution(mesh):
    sizes = {"x": 4, "y": 8, "core": 2, "z": 8}
    fine = Mesh(mesh.devices.reshape(tuple(sizes.values())), tuple(sizes))
    placed = (P(REPLICA, "z", None), P(REPLICA, "z", None), P("z", None))
    return jax.shard_map(
        functools.partial(local, sizes),
        mesh=fine,
        in_specs=placed,
        out_specs=(P(REPLICA, "z", None), P("z", None), P("z", None)),
        check_vma=False,
    )
```

```python
import functools

import jax
import jax.numpy as jnp
from jax import lax
from jax.experimental import pallas as pl
from jax.experimental.pallas import tpu as pltpu
from jax.sharding import Mesh, PartitionSpec as P

F32, BF16 = jnp.float32, jnp.bfloat16
SMEM = pl.BlockSpec(memory_space=pltpu.SMEM)
VMEM = pl.BlockSpec(memory_space=pltpu.VMEM)
HBM = pl.BlockSpec(memory_space=pltpu.HBM)
PLANE = ("x", "y")
REPLICA = ("x", "y", "core")
LIGHT = pl.CostEstimate(flops=0, bytes_accessed=0, transcendentals=0)
FULL = 60
WEIGHT = pl.CostEstimate(flops=10**11, bytes_accessed=2**21, transcendentals=0)


def merge_kernel(core_ref, grad_hbm, error_hbm, out_hbm, grad, error, merged, sems):
    parts, _, half = out_hbm.shape
    copies = []
    for i in range(parts):
        at = pl.ds(pl.multiple_of((2 * i + core_ref[0]) * half, half), half)
        copies.append(
            [
                pltpu.make_async_copy(src.at[:, at], dst.at[i], sems.at[j, i])
                for j, (src, dst) in enumerate(((grad_hbm, grad), (error_hbm, error)))
            ]
        )
        for copy in copies[-1]:
            copy.start()
    sent = []
    for i in range(parts):
        for copy in copies[i]:
            copy.wait()
        merged[i] = (grad[i].astype(F32) + error[i].astype(F32)).astype(BF16)
        sent.append(pltpu.make_async_copy(merged.at[i], out_hbm.at[i], sems.at[2, i]))
        sent[-1].start()
    for copy in sent:
        copy.wait()


def pair_kernel(keep_ref, took_ref, out_ref):
    for i in range(out_ref.shape[0]):
        out_ref[i] = keep_ref[i].astype(F32) + took_ref[i].astype(F32)


def left_kernel(factor_ref, keep_ref, took_ref, out_ref):
    height = keep_ref.shape[1]
    total = None
    for i in range(keep_ref.shape[0]):
        both = jnp.concatenate([keep_ref[i], took_ref[i]], axis=0)
        term = lax.dot_general(
            factor_ref[i], both, (((1,), (1,)), ((), ())), preferred_element_type=F32
        )
        total = term if total is None else total + term
    out_ref[...] = total[:, :height] + total[:, height:]


def gram_kernel(left_ref, out_ref):
    left = left_ref[...]
    gram = lax.dot_general(
        left, left, (((1,), (1,)), ((), ())),
        precision=lax.Precision.HIGHEST, preferred_element_type=F32,
    )
    packed = jnp.concatenate(jnp.split(gram, 2, axis=0), axis=1)
    for i in range(out_ref.shape[0]):
        out_ref[i] = packed


def factor_kernel(grams_ref, left_ref, factor_ref, round_ref):
    packed = grams_ref[0]
    for part in range(1, grams_ref.shape[0]):
        packed = packed + grams_ref[part]
    rank = packed.shape[1] // 2
    gram = jnp.concatenate([packed[:, :rank], packed[:, rank:]], axis=0)
    gram = jnp.concatenate([gram, gram], axis=1)
    blocks = rank // 8
    g = [gram[8 * n : 8 * n + 8] for n in range(blocks)]
    p = [left_ref[8 * n : 8 * n + 8, :] for n in range(blocks)]
    full = (8, 2 * rank)
    sub = lax.broadcasted_iota(jnp.int32, full, 0)

    def lane(v, k):
        return jnp.broadcast_to(v[:, k : k + 1], full)

    def row(v, k):
        return jnp.broadcast_to(v[k : k + 1, :], full)

    hold = None
    for k in range(0, rank, 4):
        own, at = k // 8, k % 8
        gs = [row(g[own], at + j) for j in range(4)]
        ps = [row(p[own], at + j) for j in range(4)]
        e = {(i, j): lane(gs[i], k + j) for i in range(4) for j in range(i, 4)}
        a, b, d = e[0, 0], e[0, 1], e[1, 1]
        det = a * d - b * b
        inverse = 1.0 / det
        ai, bi, di = a * inverse, b * inverse, d * inverse
        t00, t01 = di * e[0, 2] - bi * e[1, 2], di * e[0, 3] - bi * e[1, 3]
        t10, t11 = ai * e[1, 2] - bi * e[0, 2], ai * e[1, 3] - bi * e[0, 3]
        a2 = e[2, 2] - e[0, 2] * t00 - e[1, 2] * t10
        b2 = e[2, 3] - e[0, 2] * t01 - e[1, 2] * t11
        d2 = e[3, 3] - e[0, 3] * t01 - e[1, 3] * t11
        det2 = a2 * d2 - b2 * b2
        inverse2 = 1.0 / det2
        ai2, bi2, di2 = a2 * inverse2, b2 * inverse2, d2 * inverse2

        def solve(r):
            s2 = r[2] - t00 * r[0] - t10 * r[1]
            s3 = r[3] - t01 * r[0] - t11 * r[1]
            w2, w3 = di2 * s2 - bi2 * s3, ai2 * s3 - bi2 * s2
            q0, q1 = di * r[0] - bi * r[1], ai * r[1] - bi * r[0]
            w0, w1 = q0 - t00 * w2 - t01 * w3, q1 - t10 * w2 - t11 * w3
            return (w0, w1, w2, w3), s2, s3

        u, _, _ = solve(gs)
        v, s2, s3 = solve(ps)
        done = (
            ps[0] / jnp.sqrt(a),
            (ps[1] - (b / a) * ps[0]) / jnp.sqrt(det / a),
            s2 / jnp.sqrt(a2),
            (s3 - (b2 / a2) * s2) / jnp.sqrt(det2 / a2),
        )
        out = done[0]
        for j in range(1, 4):
            out = jnp.where(sub == at + j, done[j], out)
        if at == 0:
            hold = out
        else:
            factor_ref[8 * own : 8 * own + 8, :] = jnp.where(sub < 4, hold, out)
        for n in range(own if at == 0 else own + 1, blocks):
            c = [lane(g[n], k + j) for j in range(4)]
            if n == own:
                c = [jnp.where(sub > at + 3, x, 0.0) for x in c]
            g[n] = g[n] - (c[0] * u[0] + c[1] * u[1]) - (c[2] * u[2] + c[3] * u[3])
            p[n] = p[n] - (c[0] * v[0] + c[1] * v[1]) - (c[2] * v[2] + c[3] * v[3])
    round_ref[...] = factor_ref[...].T.astype(BF16)


def fan_kernel(place_ref, slab_ref, *out_refs):
    turned = slab_ref[...].T
    fold = turned.shape[0] // len(out_refs)
    for i in range(len(out_refs)):
        for j, out_ref in enumerate(out_refs):
            @pl.when(i == place_ref[0] ^ j)
            def _():
                out_ref[...] = turned[fold * i : fold * (i + 1)]


def right_kernel(round_ref, own_ref, *rest):
    *others, out_ref = rest
    slab = own_ref[...]
    for other in others:
        slab = slab + other[...]
    term = jnp.dot(
        slab, round_ref[...].astype(F32),
        precision=lax.Precision.HIGHEST, preferred_element_type=F32,
    )
    packed = jnp.concatenate(jnp.split(term, 2, axis=0), axis=1)
    for i in range(out_ref.shape[0]):
        out_ref[i] = packed


def decode_kernel(place_ref, round_ref, factor_ref, grad, error, *rest):
    *before, out_hbm, next_ref, out, sems = rest
    planes, fold, lanes = factor_ref.shape
    rank, half = lanes // 2, out.shape[-1]
    inner = half // (2 * fold)
    parts = planes // inner
    which = place_ref[0]
    rounded = round_ref[...]

    def factor(part):
        pieces = []
        for x in range(inner):
            piece = factor_ref[x * parts + part]
            pieces += [piece[:, :rank], piece[:, rank:]]
        return jnp.concatenate(pieces, axis=0)

    sent = []
    for i in range(parts):
        decoded = lax.dot_general(
            rounded, factor(i), (((1,), (1,)), ((), ())), preferred_element_type=F32
        )
        at = pl.ds(pl.multiple_of((2 * i + which) * half, half), half)
        out[i] = (
            grad[:, at].astype(F32) + error[:, at].astype(F32) - decoded
        ).astype(BF16)
        sent.append(pltpu.make_async_copy(out.at[i], out_hbm.at[:, at], sems.at[i]))
        sent[-1].start()
    turned = factor(place_ref[1]).astype(F32).T.astype(BF16)
    if before:
        for at, part in ((which, turned), (1 - which, before[1][...])):
            next_ref[:, pl.ds(pl.multiple_of(at * half, half), half)] = part
    else:
        next_ref[...] = turned
    for copy in sent:
        copy.wait()


def call(kernel, name, out_shape, in_specs, out_specs=VMEM, scratch_shapes=(), limit=4, cost=None, aliases=None):
    return pl.pallas_call(
        kernel,
        in_specs=in_specs,
        out_specs=out_specs,
        out_shape=out_shape,
        scratch_shapes=scratch_shapes,
        cost_estimate=cost,
        input_output_aliases=aliases or {},
        compiler_params=pltpu.CompilerParams(vmem_limit_bytes=limit * 2**20),
        name=name,
    )


def spread(block, axes, count):
    return lax.all_to_all(jnp.broadcast_to(block[None], (count, *block.shape)), axes, 0, 0)


def local(sizes, grad, error, q_in):
    across, along, shards, cores = sizes["x"], sizes["y"], sizes["z"], sizes["core"]
    planes = across * along
    replicas = planes * cores
    grad, error = grad[0], error[0]
    height, width = grad.shape
    cols, rank = q_in.shape
    half = cols // cores
    core, z = lax.axis_index("core"), lax.axis_index("z")
    swap = [(0, 1), (1, 0)]
    array = jax.ShapeDtypeStruct

    pieces = array((along, height, half), BF16)
    staged = pltpu.VMEM((height, width), BF16)

    def merge(which, name, cost):
        return call(
            merge_kernel, name, pieces, [SMEM, HBM, HBM], HBM,
            [pltpu.VMEM(pieces.shape, BF16)] * 3 + [pltpu.SemaphoreType.DMA((3, along))],
            limit=FULL, cost=cost,
        )(which.reshape(1), grad, error)

    give, keep = merge(1 - core, "give", LIGHT), merge(core, "keep", WEIGHT)
    took = lax.ppermute(give, "core", swap)
    pair = call(pair_kernel, "pair", array(pieces.shape, F32), [VMEM, VMEM], limit=8, cost=LIGHT)(keep, took)
    slab = lax.psum_scatter(pair, "y", scatter_dimension=0, tiled=True)[0]

    q_mine = lax.dynamic_slice_in_dim(q_in.T, core * half, half, 1)
    q_all = spread(q_mine, "z", shards)
    left = call(left_kernel, "left", array((rank, height), F32), [VMEM] * 3, limit=8, cost=WEIGHT)(
        q_all, keep, took
    )
    left_row = lax.all_to_all(left.reshape(replicas, -1, height), REPLICA, 0, 0).sum(0)
    left_sum = spread(left_row, REPLICA, replicas).reshape(rank, height)

    gram = call(gram_kernel, "gram", array((shards, rank // 2, 2 * rank), F32), [VMEM])(
        left_sum
    )
    grams = lax.all_to_all(gram, "z", 0, 0)
    p_factor, p_round = call(
        factor_kernel, "factor",
        [array((rank, height), F32), array((height, rank), BF16)],
        [VMEM, VMEM], [VMEM, VMEM],
    )(grams, left_sum)

    fold = half // across
    own, *give = call(
        fan_kernel, "fan", [array((fold, height), F32)] * across, [SMEM, VMEM], [VMEM] * across
    )(lax.axis_index("x").reshape(1), slab)
    others = [
        lax.ppermute(part, "x", [(i, i ^ j) for i in range(across)])
        for j, part in enumerate(give, 1)
    ]
    term = call(
        right_kernel, "right", array((shards, fold // 2, 2 * rank), F32), [VMEM] * (1 + across)
    )(p_round, own, *others)
    q_mine = (lax.all_to_all(term, "z", 0, 0).sum(0) / replicas).astype(BF16)
    q_own = spread(q_mine, PLANE, planes)
    q_other = lax.ppermute(q_own, "core", swap)


    def decode(which, name, factor, *before):
        return call(
            decode_kernel, name,
            [array((height, width), BF16), array((rank, cols if before else half), BF16)],
            [SMEM] + [VMEM] * 4 + ([HBM, VMEM] if before else []), [HBM, VMEM],
            [pltpu.VMEM(pieces.shape, BF16), pltpu.SemaphoreType.DMA((along,))],
            limit=12, aliases={5: 0} if before else None,
        )(jnp.stack([which, z]), p_round, factor, grad, error, *before)

    new_error, q_next = decode(1 - core, "other", q_other, *decode(core, "own", q_own))
    return new_error[None], p_factor.T, q_next.T


def solution(mesh):
    sizes = {"x": 4, "y": 8, "core": 2, "z": 8}
    fine = Mesh(mesh.devices.reshape(tuple(sizes.values())), tuple(sizes))
    placed = (P(REPLICA, "z", None), P(REPLICA, "z", None), P("z", None))
    return jax.shard_map(
        functools.partial(local, sizes),
        mesh=fine,
        in_specs=placed,
        out_specs=(P(REPLICA, "z", None), P("z", None), P("z", None)),
        check_vma=False,
    )
```

```python
import functools

import jax
import jax.numpy as jnp
from jax import lax
from jax.experimental import pallas as pl
from jax.experimental.pallas import tpu as pltpu
from jax.sharding import Mesh, PartitionSpec as P

F32, BF16 = jnp.float32, jnp.bfloat16
SMEM = pl.BlockSpec(memory_space=pltpu.SMEM)
VMEM = pl.BlockSpec(memory_space=pltpu.VMEM)
HBM = pl.BlockSpec(memory_space=pltpu.HBM)
PLANE = ("x", "y")
REPLICA = ("x", "y", "core")
LIGHT = pl.CostEstimate(flops=0, bytes_accessed=0, transcendentals=0)
WEIGHT = pl.CostEstimate(flops=10**11, bytes_accessed=2**21, transcendentals=0)


def merge_kernel(core_ref, grad, error, out_ref):
    parts, _, half = out_ref.shape
    for i in range(parts):
        at = pl.ds(pl.multiple_of((2 * i + core_ref[0]) * half, half), half)
        out_ref[i] = (grad[:, at].astype(F32) + error[:, at].astype(F32)).astype(BF16)


def halve_kernel(bit_ref, hold_ref, took_ref, hold_out, give_out):
    many = hold_out.shape[0]
    for out, bit in ((give_out, 1 - bit_ref[0]), (hold_out, bit_ref[0])):
        for j in range(many):
            i = bit * many + j
            out[j] = hold_ref[i].astype(F32) + took_ref[i].astype(F32)


def turn_kernel(bit_ref, hold_ref, took_ref, hold_out, give_out):
    turned = (hold_ref[0] + took_ref[0]).T
    many = turned.shape[0] // 2
    low, high = turned[:many], turned[many:]

    @pl.when(bit_ref[0] == 0)
    def _():
        hold_out[0], give_out[0] = low, high

    @pl.when(bit_ref[0] != 0)
    def _():
        hold_out[0], give_out[0] = high, low


def split_kernel(bit_ref, hold_ref, took_ref, hold_out, give_out):
    many = hold_out.shape[1]
    for out, bit in ((give_out, 1 - bit_ref[0]), (hold_out, bit_ref[0])):
        at = pl.ds(pl.multiple_of(bit * many, many), many)
        out[0] = hold_ref[0, at, :] + took_ref[0, at, :]


def left_kernel(factor_ref, keep_ref, took_ref, out_ref):
    height = keep_ref.shape[1]
    total = None
    for i in range(keep_ref.shape[0]):
        both = jnp.concatenate([keep_ref[i], took_ref[i]], axis=0)
        term = lax.dot_general(
            factor_ref[i], both, (((1,), (1,)), ((), ())), preferred_element_type=F32
        )
        total = term if total is None else total + term
    out_ref[...] = total[:, :height] + total[:, height:]


def gram_kernel(left_ref, out_ref):
    left = left_ref[...]
    gram = lax.dot_general(
        left, left, (((1,), (1,)), ((), ())),
        precision=lax.Precision.HIGHEST, preferred_element_type=F32,
    )
    packed = jnp.concatenate(jnp.split(gram, 2, axis=0), axis=1)
    for i in range(out_ref.shape[0]):
        out_ref[i] = packed


def factor_kernel(grams_ref, left_ref, factor_ref, round_ref):
    packed = grams_ref[0]
    for part in range(1, grams_ref.shape[0]):
        packed = packed + grams_ref[part]
    rank = packed.shape[1] // 2
    gram = jnp.concatenate([packed[:, :rank], packed[:, rank:]], axis=0)
    gram = jnp.concatenate([gram, gram], axis=1)
    blocks = rank // 8
    g = [gram[8 * n : 8 * n + 8] for n in range(blocks)]
    p = [left_ref[8 * n : 8 * n + 8, :] for n in range(blocks)]
    full = (8, 2 * rank)
    sub = lax.broadcasted_iota(jnp.int32, full, 0)

    def lane(v, k):
        return jnp.broadcast_to(v[:, k : k + 1], full)

    def row(v, k):
        return jnp.broadcast_to(v[k : k + 1, :], full)

    hold = None
    for k in range(0, rank, 4):
        own, at = k // 8, k % 8
        gs = [row(g[own], at + j) for j in range(4)]
        ps = [row(p[own], at + j) for j in range(4)]
        e = {(i, j): lane(gs[i], k + j) for i in range(4) for j in range(i, 4)}
        a, b, d = e[0, 0], e[0, 1], e[1, 1]
        det = a * d - b * b
        inverse = 1.0 / det
        ai, bi, di = a * inverse, b * inverse, d * inverse
        t00, t01 = di * e[0, 2] - bi * e[1, 2], di * e[0, 3] - bi * e[1, 3]
        t10, t11 = ai * e[1, 2] - bi * e[0, 2], ai * e[1, 3] - bi * e[0, 3]
        a2 = e[2, 2] - e[0, 2] * t00 - e[1, 2] * t10
        b2 = e[2, 3] - e[0, 2] * t01 - e[1, 2] * t11
        d2 = e[3, 3] - e[0, 3] * t01 - e[1, 3] * t11
        det2 = a2 * d2 - b2 * b2
        inverse2 = 1.0 / det2
        ai2, bi2, di2 = a2 * inverse2, b2 * inverse2, d2 * inverse2

        def solve(r):
            s2 = r[2] - t00 * r[0] - t10 * r[1]
            s3 = r[3] - t01 * r[0] - t11 * r[1]
            w2, w3 = di2 * s2 - bi2 * s3, ai2 * s3 - bi2 * s2
            q0, q1 = di * r[0] - bi * r[1], ai * r[1] - bi * r[0]
            w0, w1 = q0 - t00 * w2 - t01 * w3, q1 - t10 * w2 - t11 * w3
            return (w0, w1, w2, w3), s2, s3

        u, _, _ = solve(gs)
        v, s2, s3 = solve(ps)
        done = (
            ps[0] / jnp.sqrt(a),
            (ps[1] - (b / a) * ps[0]) / jnp.sqrt(det / a),
            s2 / jnp.sqrt(a2),
            (s3 - (b2 / a2) * s2) / jnp.sqrt(det2 / a2),
        )
        out = done[0]
        for j in range(1, 4):
            out = jnp.where(sub == at + j, done[j], out)
        if at == 0:
            hold = out
        else:
            factor_ref[8 * own : 8 * own + 8, :] = jnp.where(sub < 4, hold, out)
        for n in range(own if at == 0 else own + 1, blocks):
            c = [lane(g[n], k + j) for j in range(4)]
            if n == own:
                c = [jnp.where(sub > at + 3, x, 0.0) for x in c]
            g[n] = g[n] - (c[0] * u[0] + c[1] * u[1]) - (c[2] * u[2] + c[3] * u[3])
            p[n] = p[n] - (c[0] * v[0] + c[1] * v[1]) - (c[2] * v[2] + c[3] * v[3])
    round_ref[...] = factor_ref[...].T.astype(BF16)


def right_kernel(round_ref, hold_ref, took_ref, out_ref):
    term = jnp.dot(
        hold_ref[0] + took_ref[0], round_ref[...].astype(F32),
        precision=lax.Precision.HIGHEST, preferred_element_type=F32,
    )
    packed = jnp.concatenate(jnp.split(term, 2, axis=0), axis=1)
    for i in range(out_ref.shape[0]):
        out_ref[i] = packed


def decode_kernel(place_ref, round_ref, factor_ref, grad, error, *rest):
    *before, out_hbm, next_ref, out, sems = rest
    planes, fold, lanes = factor_ref.shape
    rank, half = lanes // 2, out.shape[-1]
    inner = half // (2 * fold)
    parts = planes // inner
    which = place_ref[0]
    rounded = round_ref[...]

    def factor(part):
        pieces = []
        for x in range(inner):
            piece = factor_ref[owner(part, x)]
            pieces += [piece[:, :rank], piece[:, rank:]]
        return jnp.concatenate(pieces, axis=0)

    sent = []
    for i in range(parts):
        decoded = lax.dot_general(
            rounded, factor(i), (((1,), (1,)), ((), ())), preferred_element_type=F32
        )
        at = pl.ds(pl.multiple_of((2 * i + which) * half, half), half)
        out[i] = (
            grad[:, at].astype(F32) + error[:, at].astype(F32) - decoded
        ).astype(BF16)
        sent.append(pltpu.make_async_copy(out.at[i], out_hbm.at[:, at], sems.at[i]))
        sent[-1].start()
    turned = factor(place_ref[1]).astype(F32).T.astype(BF16)
    if before:
        for at, part in ((which, turned), (1 - which, before[1][...])):
            next_ref[:, pl.ds(pl.multiple_of(at * half, half), half)] = part
    else:
        next_ref[...] = turned
    for copy in sent:
        copy.wait()


def owner(block, quarter):
    x = block // 4 + 2 * (block // 2 % 2)
    y = block % 2 + 2 * (quarter // 2) + 4 * (quarter % 2)
    return 8 * x + y


def call(kernel, name, out_shape, in_specs, out_specs=VMEM, scratch_shapes=(), limit=4, cost=None, aliases=None):
    return pl.pallas_call(
        kernel,
        in_specs=in_specs,
        out_specs=out_specs,
        out_shape=out_shape,
        scratch_shapes=scratch_shapes,
        cost_estimate=cost,
        input_output_aliases=aliases or {},
        compiler_params=pltpu.CompilerParams(vmem_limit_bytes=limit * 2**20),
        name=name,
    )


def spread(block, axes, count):
    return lax.all_to_all(jnp.broadcast_to(block[None], (count, *block.shape)), axes, 0, 0)


def local(sizes, grad, error, q_in):
    planes, shards, cores = sizes["x"] * sizes["y"], sizes["z"], sizes["core"]
    replicas = planes * cores
    grad, error = grad[0], error[0]
    height, width = grad.shape
    cols, rank = q_in.shape
    half = cols // cores
    core, z = lax.axis_index("core"), lax.axis_index("z")
    swap = [(0, 1), (1, 0)]
    array = jax.ShapeDtypeStruct

    blocks = width // cols
    pieces = array((blocks, height, half), BF16)

    def merge(which, name, cost):
        return call(
            merge_kernel, name, pieces, [SMEM, VMEM, VMEM], limit=12, cost=cost
        )(which.reshape(1), grad, error)

    give, keep = merge(1 - core, "give", LIGHT), merge(core, "keep", WEIGHT)
    took = lax.ppermute(give, "core", swap)

    def halve(kernel, name, axis, bit, hold, took, shape):
        place = (lax.axis_index(axis) // bit % 2).reshape(1)
        out = array(shape, F32)
        return call(kernel, name, [out, out], [SMEM, VMEM, VMEM], [VMEM, VMEM], limit=8)(
            place, hold, took
        )

    def trade(give, axis, bit):
        return lax.ppermute(give, axis, [(i, i ^ bit) for i in range(sizes[axis])])

    def after(first, *then):
        return lax.optimization_barrier((first, *then))

    hold, give = halve(
        halve_kernel, "pair", "x", 1, keep, took, (blocks // 2, height, half)
    )
    took_a = trade(give, "x", 1)

    q_mine = lax.dynamic_slice_in_dim(q_in.T, core * half, half, 1)
    q_all = spread(q_mine, "z", shards)
    q_all, hold = after(q_all, hold)
    left = call(left_kernel, "left", array((rank, height), F32), [VMEM] * 3, limit=8, cost=WEIGHT)(
        q_all, keep, took
    )
    left_row = lax.all_to_all(left.reshape(replicas, -1, height), REPLICA, 0, 0).sum(0)
    hold, give = halve(
        halve_kernel, "halve_x", "x", 2, hold, took_a, (blocks // 4, height, half)
    )
    left_row, hold, give = after(left_row, hold, give)
    took_b = trade(give, "x", 2)
    left_sum = spread(left_row, REPLICA, replicas).reshape(rank, height)
    hold, give = halve(
        halve_kernel, "halve_y", "y", 1, hold, took_b, (blocks // 8, height, half)
    )
    left_sum, hold, give = after(left_sum, hold, give)
    took_c = trade(give, "y", 1)

    gram = call(gram_kernel, "gram", array((shards, rank // 2, 2 * rank), F32), [VMEM])(
        left_sum
    )
    grams = lax.all_to_all(gram, "z", 0, 0)
    hold, give = halve(
        turn_kernel, "turn", "y", 2, hold, took_c, (1, half // 2, height)
    )
    took_d = trade(give, "y", 2)
    hold, give = halve(
        split_kernel, "split", "y", 4, hold, took_d, (1, half // 4, height)
    )
    took_e = trade(give, "y", 4)
    p_factor, p_round = call(
        factor_kernel, "factor",
        [array((rank, height), F32), array((height, rank), BF16)],
        [VMEM, VMEM], [VMEM, VMEM],
    )(grams, left_sum)

    fold = half // 4
    term = call(
        right_kernel, "right", array((shards, fold // 2, 2 * rank), F32), [VMEM] * 3
    )(p_round, hold, took_e)
    q_mine = (lax.all_to_all(term, "z", 0, 0).sum(0) / replicas).astype(BF16)
    q_own = spread(q_mine, PLANE, planes)
    q_other = lax.ppermute(q_own, "core", swap)


    def decode(which, name, factor, *before):
        return call(
            decode_kernel, name,
            [array((height, width), BF16), array((rank, cols if before else half), BF16)],
            [SMEM] + [VMEM] * 4 + ([HBM, VMEM] if before else []), [HBM, VMEM],
            [pltpu.VMEM(pieces.shape, BF16), pltpu.SemaphoreType.DMA((blocks,))],
            limit=12, aliases={5: 0} if before else None,
        )(jnp.stack([which, z]), p_round, factor, grad, error, *before)

    new_error, q_next = decode(1 - core, "other", q_other, *decode(core, "own", q_own))
    return new_error[None], p_factor.T, q_next.T


def solution(mesh):
    sizes = {"x": 4, "y": 8, "core": 2, "z": 8}
    fine = Mesh(mesh.devices.reshape(tuple(sizes.values())), tuple(sizes))
    placed = (P(REPLICA, "z", None), P(REPLICA, "z", None), P("z", None))
    return jax.shard_map(
        functools.partial(local, sizes),
        mesh=fine,
        in_specs=placed,
        out_specs=(P(REPLICA, "z", None), P("z", None), P("z", None)),
        check_vma=False,
    )
```

```python
import functools

import jax
import jax.numpy as jnp
from jax import lax
from jax.experimental import pallas as pl
from jax.experimental.pallas import tpu as pltpu
from jax.sharding import Mesh, PartitionSpec as P

F32, BF16 = jnp.float32, jnp.bfloat16
SMEM = pl.BlockSpec(memory_space=pltpu.SMEM)
VMEM = pl.BlockSpec(memory_space=pltpu.VMEM)
HBM = pl.BlockSpec(memory_space=pltpu.HBM)
PLANE = ("x", "y")
REPLICA = ("x", "y", "core")
LIGHT = pl.CostEstimate(flops=0, bytes_accessed=0, transcendentals=0)
FULL, MOST = 60, 52
WEIGHT = pl.CostEstimate(flops=10**11, bytes_accessed=2**21, transcendentals=0)


def merge_kernel(core_ref, grad_hbm, error_hbm, out_ref, grad, error, sems):
    parts, _, half = out_ref.shape
    copies = []
    for i in range(parts):
        at = pl.ds(pl.multiple_of((2 * i + core_ref[0]) * half, half), half)
        copies.append(
            [
                pltpu.make_async_copy(src.at[:, at], dst.at[i], sems.at[j, i])
                for j, (src, dst) in enumerate(((grad_hbm, grad), (error_hbm, error)))
            ]
        )
        for copy in copies[-1]:
            copy.start()
    for i in range(parts):
        for copy in copies[i]:
            copy.wait()
        out_ref[i] = (grad[i].astype(F32) + error[i].astype(F32)).astype(BF16)


def pair_kernel(keep_ref, took_ref, out_ref):
    for i in range(out_ref.shape[0]):
        out_ref[i] = (keep_ref[i].astype(F32) + took_ref[i].astype(F32)).T


def slots_kernel(core_ref, factor_hbm, out_ref, sems):
    many, _, half = out_ref.shape
    at = pl.ds(pl.multiple_of(core_ref[0] * half, half), half)
    copies = [
        pltpu.make_async_copy(factor_hbm.at[:, at], out_ref.at[i], sems.at[i])
        for i in range(many)
    ]
    for copy in copies:
        copy.start()
    for copy in copies:
        copy.wait()


def left_kernel(factor_ref, keep_ref, took_ref, out_ref):
    height = keep_ref.shape[1]
    total = None
    for i in range(keep_ref.shape[0]):
        both = jnp.concatenate([keep_ref[i], took_ref[i]], axis=0)
        term = lax.dot_general(
            factor_ref[i], both, (((1,), (1,)), ((), ())), preferred_element_type=F32
        )
        total = term if total is None else total + term
    out_ref[...] = total[:, :height] + total[:, height:]


def gram_kernel(left_ref, out_ref):
    left = left_ref[...]
    gram = lax.dot_general(
        left, left, (((1,), (1,)), ((), ())),
        precision=lax.Precision.HIGHEST, preferred_element_type=F32,
    )
    packed = jnp.concatenate(jnp.split(gram, 2, axis=0), axis=1)
    for i in range(out_ref.shape[0]):
        out_ref[i] = packed


def factor_kernel(grams_ref, left_ref, factor_ref, round_ref):
    packed = grams_ref[0]
    for part in range(1, grams_ref.shape[0]):
        packed = packed + grams_ref[part]
    rank = packed.shape[1] // 2
    gram = jnp.concatenate([packed[:, :rank], packed[:, rank:]], axis=0)
    gram = jnp.concatenate([gram, gram], axis=1)
    blocks = rank // 8
    g = [gram[8 * n : 8 * n + 8] for n in range(blocks)]
    p = [left_ref[8 * n : 8 * n + 8, :] for n in range(blocks)]
    full = (8, 2 * rank)
    sub = lax.broadcasted_iota(jnp.int32, full, 0)

    def lane(v, k):
        return jnp.broadcast_to(v[:, k : k + 1], full)

    def row(v, k):
        return jnp.broadcast_to(v[k : k + 1, :], full)

    hold = None
    for k in range(0, rank, 4):
        own, at = k // 8, k % 8
        gs = [row(g[own], at + j) for j in range(4)]
        ps = [row(p[own], at + j) for j in range(4)]
        e = {(i, j): lane(gs[i], k + j) for i in range(4) for j in range(i, 4)}
        a, b, d = e[0, 0], e[0, 1], e[1, 1]
        det = a * d - b * b
        inverse = 1.0 / det
        ai, bi, di = a * inverse, b * inverse, d * inverse
        t00, t01 = di * e[0, 2] - bi * e[1, 2], di * e[0, 3] - bi * e[1, 3]
        t10, t11 = ai * e[1, 2] - bi * e[0, 2], ai * e[1, 3] - bi * e[0, 3]
        a2 = e[2, 2] - e[0, 2] * t00 - e[1, 2] * t10
        b2 = e[2, 3] - e[0, 2] * t01 - e[1, 2] * t11
        d2 = e[3, 3] - e[0, 3] * t01 - e[1, 3] * t11
        det2 = a2 * d2 - b2 * b2
        inverse2 = 1.0 / det2
        ai2, bi2, di2 = a2 * inverse2, b2 * inverse2, d2 * inverse2

        def solve(r):
            s2 = r[2] - t00 * r[0] - t10 * r[1]
            s3 = r[3] - t01 * r[0] - t11 * r[1]
            w2, w3 = di2 * s2 - bi2 * s3, ai2 * s3 - bi2 * s2
            q0, q1 = di * r[0] - bi * r[1], ai * r[1] - bi * r[0]
            w0, w1 = q0 - t00 * w2 - t01 * w3, q1 - t10 * w2 - t11 * w3
            return (w0, w1, w2, w3), s2, s3

        u, _, _ = solve(gs)
        v, s2, s3 = solve(ps)
        done = (
            ps[0] / jnp.sqrt(a),
            (ps[1] - (b / a) * ps[0]) / jnp.sqrt(det / a),
            s2 / jnp.sqrt(a2),
            (s3 - (b2 / a2) * s2) / jnp.sqrt(det2 / a2),
        )
        out = done[0]
        for j in range(1, 4):
            out = jnp.where(sub == at + j, done[j], out)
        if at == 0:
            hold = out
        else:
            factor_ref[8 * own : 8 * own + 8, :] = jnp.where(sub < 4, hold, out)
        for n in range(own if at == 0 else own + 1, blocks):
            c = [lane(g[n], k + j) for j in range(4)]
            if n == own:
                c = [jnp.where(sub > at + 3, x, 0.0) for x in c]
            g[n] = g[n] - (c[0] * u[0] + c[1] * u[1]) - (c[2] * u[2] + c[3] * u[3])
            p[n] = p[n] - (c[0] * v[0] + c[1] * v[1]) - (c[2] * v[2] + c[3] * v[3])
    round_ref[...] = factor_ref[...].T.astype(BF16)


def right_kernel(slab_ref, round_ref, out_ref):
    slab = slab_ref[0]
    for i in range(1, slab_ref.shape[0]):
        slab = slab + slab_ref[i]
    term = jnp.dot(
        slab, round_ref[...].astype(F32),
        precision=lax.Precision.HIGHEST, preferred_element_type=F32,
    )
    packed = jnp.concatenate(jnp.split(term, 2, axis=0), axis=1)
    for i in range(out_ref.shape[0]):
        out_ref[i] = packed


def decode_kernel(place_ref, round_ref, factor_ref, grad, error, *rest):
    *before, out_hbm, next_ref, out, sems = rest
    planes, fold, lanes = factor_ref.shape
    rank, half = lanes // 2, out.shape[-1]
    inner = half // (2 * fold)
    parts = planes // inner
    which = place_ref[0]
    rounded = round_ref[...]

    def factor(part):
        pieces = []
        for x in range(inner):
            piece = factor_ref[x * parts + part]
            pieces += [piece[:, :rank], piece[:, rank:]]
        return jnp.concatenate(pieces, axis=0)

    sent = []
    for i in range(parts):
        decoded = lax.dot_general(
            rounded, factor(i), (((1,), (1,)), ((), ())), preferred_element_type=F32
        )
        at = pl.ds(pl.multiple_of((2 * i + which) * half, half), half)
        out[i] = (
            grad[:, at].astype(F32) + error[:, at].astype(F32) - decoded
        ).astype(BF16)
        sent.append(pltpu.make_async_copy(out.at[i], out_hbm.at[:, at], sems.at[i]))
        sent[-1].start()
    turned = factor(place_ref[1]).astype(F32).T.astype(BF16)
    if before:
        for at, part in ((which, turned), (1 - which, before[1][...])):
            next_ref[:, pl.ds(pl.multiple_of(at * half, half), half)] = part
    else:
        next_ref[...] = turned
    for copy in sent:
        copy.wait()


def call(kernel, name, out_shape, in_specs, out_specs=VMEM, scratch_shapes=(), limit=4, cost=None, aliases=None):
    return pl.pallas_call(
        kernel,
        in_specs=in_specs,
        out_specs=out_specs,
        out_shape=out_shape,
        scratch_shapes=scratch_shapes,
        cost_estimate=cost,
        input_output_aliases=aliases or {},
        compiler_params=pltpu.CompilerParams(vmem_limit_bytes=limit * 2**20),
        name=name,
    )


def spread(block, axes, count):
    return lax.all_to_all(jnp.broadcast_to(block[None], (count, *block.shape)), axes, 0, 0)


def local(sizes, grad, error, q_in):
    across, along, shards, cores = sizes["x"], sizes["y"], sizes["z"], sizes["core"]
    planes = across * along
    replicas = planes * cores
    grad, error = grad[0], error[0]
    height, width = grad.shape
    cols, rank = q_in.shape
    half = cols // cores
    core, z = lax.axis_index("core"), lax.axis_index("z")
    swap = [(0, 1), (1, 0)]
    array = jax.ShapeDtypeStruct

    pieces = array((along, height, half), BF16)
    staged = pltpu.VMEM((height, width), BF16)

    def merge(which, name, cost):
        return call(
            merge_kernel, name, pieces, [SMEM, HBM, HBM], VMEM,
            [pltpu.VMEM(pieces.shape, BF16)] * 2 + [pltpu.SemaphoreType.DMA((2, along))],
            limit=MOST, cost=cost,
        )(which.reshape(1), grad, error)

    give, keep = merge(1 - core, "give", LIGHT), merge(core, "keep", WEIGHT)
    took = lax.ppermute(give, "core", swap)
    pair = call(pair_kernel, "pair", array((along, half, height), F32), [VMEM, VMEM], limit=12, cost=LIGHT)(keep, took)
    slab = lax.psum_scatter(pair, "y", scatter_dimension=0, tiled=True)[0]

    q_mine = call(
        slots_kernel, "slots", array((shards, rank, half), BF16), [SMEM, HBM], VMEM,
        [pltpu.SemaphoreType.DMA((shards,))], limit=FULL,
    )(core.reshape(1), q_in.T)
    q_all = lax.all_to_all(q_mine, "z", 0, 0)
    left = call(left_kernel, "left", array((rank, height), F32), [VMEM] * 3, limit=8, cost=WEIGHT)(
        q_all, keep, took
    )
    left_row = lax.all_to_all(left.reshape(replicas, -1, height), REPLICA, 0, 0).sum(0)
    left_sum = spread(left_row, REPLICA, replicas).reshape(rank, height)

    gram = call(gram_kernel, "gram", array((shards, rank // 2, 2 * rank), F32), [VMEM])(
        left_sum
    )
    grams = lax.all_to_all(gram, "z", 0, 0)
    p_factor, p_round = call(
        factor_kernel, "factor",
        [array((rank, height), F32), array((height, rank), BF16)],
        [VMEM, VMEM], [VMEM, VMEM],
    )(grams, left_sum)

    fold = half // across
    slab = lax.all_to_all(slab.reshape(across, fold, height), "x", 0, 0)
    term = call(
        right_kernel, "right", array((shards, fold // 2, 2 * rank), F32), [VMEM, VMEM]
    )(slab, p_round)
    q_mine = (lax.all_to_all(term, "z", 0, 0).sum(0) / replicas).astype(BF16)
    q_own = spread(q_mine, PLANE, planes)
    q_other = lax.ppermute(q_own, "core", swap)


    def decode(which, name, factor, *before):
        return call(
            decode_kernel, name,
            [array((height, width), BF16), array((rank, cols if before else half), BF16)],
            [SMEM] + [VMEM] * 4 + ([HBM, VMEM] if before else []), [HBM, VMEM],
            [pltpu.VMEM(pieces.shape, BF16), pltpu.SemaphoreType.DMA((along,))],
            limit=12, aliases={5: 0} if before else None,
        )(jnp.stack([which, z]), p_round, factor, grad, error, *before)

    new_error, q_next = decode(1 - core, "other", q_other, *decode(core, "own", q_own))
    return new_error[None], p_factor.T, q_next.T


def solution(mesh):
    sizes = {"x": 4, "y": 8, "core": 2, "z": 8}
    fine = Mesh(mesh.devices.reshape(tuple(sizes.values())), tuple(sizes))
    placed = (P(REPLICA, "z", None), P(REPLICA, "z", None), P("z", None))
    return jax.shard_map(
        functools.partial(local, sizes),
        mesh=fine,
        in_specs=placed,
        out_specs=(P(REPLICA, "z", None), P("z", None), P("z", None)),
        check_vma=False,
    )
```

```python
import functools

import jax
import jax.numpy as jnp
from jax import lax
from jax.experimental import pallas as pl
from jax.experimental.pallas import tpu as pltpu
from jax.sharding import Mesh, PartitionSpec as P

F32, BF16 = jnp.float32, jnp.bfloat16
SMEM = pl.BlockSpec(memory_space=pltpu.SMEM)
VMEM = pl.BlockSpec(memory_space=pltpu.VMEM)
HBM = pl.BlockSpec(memory_space=pltpu.HBM)
PLANE = ("x", "y")
REPLICA = ("x", "y", "core")
LIGHT = pl.CostEstimate(flops=0, bytes_accessed=0, transcendentals=0)
FULL, MOST = 60, 52
WEIGHT = pl.CostEstimate(flops=10**11, bytes_accessed=2**21, transcendentals=0)


def merge_kernel(core_ref, grad_hbm, error_hbm, out_ref, grad, error, sems):
    parts, _, half = out_ref.shape
    copies = []
    for i in range(parts):
        at = pl.ds(pl.multiple_of((2 * i + core_ref[0]) * half, half), half)
        copies.append(
            [
                pltpu.make_async_copy(src.at[:, at], dst.at[i], sems.at[j, i])
                for j, (src, dst) in enumerate(((grad_hbm, grad), (error_hbm, error)))
            ]
        )
        for copy in copies[-1]:
            copy.start()
    for i in range(parts):
        for copy in copies[i]:
            copy.wait()
        out_ref[i] = (grad[i].astype(F32) + error[i].astype(F32)).astype(BF16)


def pair_kernel(keep_ref, took_ref, out_ref):
    for i in range(out_ref.shape[0]):
        out_ref[i] = (keep_ref[i].astype(F32) + took_ref[i].astype(F32)).T


def slots_kernel(core_ref, factor_hbm, out_hbm, sems):
    many, _, half = out_hbm.shape
    at = pl.ds(pl.multiple_of(core_ref[0] * half, half), half)
    copies = [
        pltpu.make_async_copy(factor_hbm.at[:, at], out_hbm.at[i], sems.at[i])
        for i in range(many)
    ]
    for copy in copies:
        copy.start()
    for copy in copies:
        copy.wait()


def left_kernel(factor_ref, keep_ref, took_ref, out_ref):
    height = keep_ref.shape[1]
    total = None
    for i in range(keep_ref.shape[0]):
        both = jnp.concatenate([keep_ref[i], took_ref[i]], axis=0)
        term = lax.dot_general(
            factor_ref[i], both, (((1,), (1,)), ((), ())), preferred_element_type=F32
        )
        total = term if total is None else total + term
    total = total[:, :height] + total[:, height:]
    for i in range(out_ref.shape[0]):
        out_ref[i] = total


def sum_kernel(parts_ref, out_ref):
    total = parts_ref[0]
    for i in range(1, parts_ref.shape[0]):
        total = total + parts_ref[i]
    for i in range(out_ref.shape[0]):
        out_ref[i] = total


def gram_kernel(parts_ref, left_ref, out_ref):
    left = parts_ref[0]
    for i in range(1, parts_ref.shape[0]):
        left = left + parts_ref[i]
    left_ref[...] = left
    gram = lax.dot_general(
        left, left, (((1,), (1,)), ((), ())),
        precision=lax.Precision.HIGHEST, preferred_element_type=F32,
    )
    packed = jnp.concatenate(jnp.split(gram, 2, axis=0), axis=1)
    for i in range(out_ref.shape[0]):
        out_ref[i] = packed


def factor_kernel(grams_ref, left_ref, factor_ref, round_ref):
    packed = grams_ref[0]
    for part in range(1, grams_ref.shape[0]):
        packed = packed + grams_ref[part]
    rank = packed.shape[1] // 2
    gram = jnp.concatenate([packed[:, :rank], packed[:, rank:]], axis=0)
    gram = jnp.concatenate([gram, gram], axis=1)
    blocks = rank // 8
    g = [gram[8 * n : 8 * n + 8] for n in range(blocks)]
    p = [left_ref[8 * n : 8 * n + 8, :] for n in range(blocks)]
    full = (8, 2 * rank)
    sub = lax.broadcasted_iota(jnp.int32, full, 0)

    def lane(v, k):
        return jnp.broadcast_to(v[:, k : k + 1], full)

    def row(v, k):
        return jnp.broadcast_to(v[k : k + 1, :], full)

    hold = None
    for k in range(0, rank, 4):
        own, at = k // 8, k % 8
        gs = [row(g[own], at + j) for j in range(4)]
        ps = [row(p[own], at + j) for j in range(4)]
        e = {(i, j): lane(gs[i], k + j) for i in range(4) for j in range(i, 4)}
        a, b, d = e[0, 0], e[0, 1], e[1, 1]
        det = a * d - b * b
        inverse = 1.0 / det
        ai, bi, di = a * inverse, b * inverse, d * inverse
        t00, t01 = di * e[0, 2] - bi * e[1, 2], di * e[0, 3] - bi * e[1, 3]
        t10, t11 = ai * e[1, 2] - bi * e[0, 2], ai * e[1, 3] - bi * e[0, 3]
        a2 = e[2, 2] - e[0, 2] * t00 - e[1, 2] * t10
        b2 = e[2, 3] - e[0, 2] * t01 - e[1, 2] * t11
        d2 = e[3, 3] - e[0, 3] * t01 - e[1, 3] * t11
        det2 = a2 * d2 - b2 * b2
        inverse2 = 1.0 / det2
        ai2, bi2, di2 = a2 * inverse2, b2 * inverse2, d2 * inverse2

        def solve(r):
            s2 = r[2] - t00 * r[0] - t10 * r[1]
            s3 = r[3] - t01 * r[0] - t11 * r[1]
            w2, w3 = di2 * s2 - bi2 * s3, ai2 * s3 - bi2 * s2
            q0, q1 = di * r[0] - bi * r[1], ai * r[1] - bi * r[0]
            w0, w1 = q0 - t00 * w2 - t01 * w3, q1 - t10 * w2 - t11 * w3
            return (w0, w1, w2, w3), s2, s3

        u, _, _ = solve(gs)
        v, s2, s3 = solve(ps)
        done = (
            ps[0] / jnp.sqrt(a),
            (ps[1] - (b / a) * ps[0]) / jnp.sqrt(det / a),
            s2 / jnp.sqrt(a2),
            (s3 - (b2 / a2) * s2) / jnp.sqrt(det2 / a2),
        )
        out = done[0]
        for j in range(1, 4):
            out = jnp.where(sub == at + j, done[j], out)
        if at == 0:
            hold = out
        else:
            factor_ref[8 * own : 8 * own + 8, :] = jnp.where(sub < 4, hold, out)
        for n in range(own if at == 0 else own + 1, blocks):
            c = [lane(g[n], k + j) for j in range(4)]
            if n == own:
                c = [jnp.where(sub > at + 3, x, 0.0) for x in c]
            g[n] = g[n] - (c[0] * u[0] + c[1] * u[1]) - (c[2] * u[2] + c[3] * u[3])
            p[n] = p[n] - (c[0] * v[0] + c[1] * v[1]) - (c[2] * v[2] + c[3] * v[3])
    round_ref[...] = factor_ref[...].T.astype(BF16)


def right_kernel(slab_ref, round_ref, out_ref):
    slab = slab_ref[0]
    for i in range(1, slab_ref.shape[0]):
        slab = slab + slab_ref[i]
    term = jnp.dot(
        slab, round_ref[...].astype(F32),
        precision=lax.Precision.HIGHEST, preferred_element_type=F32,
    )
    packed = jnp.concatenate(jnp.split(term, 2, axis=0), axis=1)
    for i in range(out_ref.shape[0]):
        out_ref[i] = packed


def decode_kernel(place_ref, round_ref, factor_ref, grad, error, *rest):
    *before, out_hbm, next_hbm, out, turned, sems = rest
    planes, fold, lanes = factor_ref.shape
    rank, half = lanes // 2, out.shape[-1]
    inner = half // (2 * fold)
    parts = planes // inner
    which = place_ref[0]
    rounded = round_ref[...]

    def factor(part):
        pieces = []
        for x in range(inner):
            piece = factor_ref[x * parts + part]
            pieces += [piece[:, :rank], piece[:, rank:]]
        return jnp.concatenate(pieces, axis=0)

    mine = factor(place_ref[1]).astype(F32).T.astype(BF16)
    if before:
        for at, part in ((which, mine), (1 - which, before[1][...])):
            turned[:, pl.ds(pl.multiple_of(at * half, half), half)] = part
    else:
        turned[...] = mine
    sent = [pltpu.make_async_copy(turned, next_hbm, sems.at[parts])]
    sent[-1].start()
    for i in range(parts):
        decoded = lax.dot_general(
            rounded, factor(i), (((1,), (1,)), ((), ())), preferred_element_type=F32
        )
        at = pl.ds(pl.multiple_of((2 * i + which) * half, half), half)
        out[i] = (
            grad[:, at].astype(F32) + error[:, at].astype(F32) - decoded
        ).astype(BF16)
        sent.append(pltpu.make_async_copy(out.at[i], out_hbm.at[:, at], sems.at[i]))
        sent[-1].start()
    for copy in sent:
        copy.wait()


def call(kernel, name, out_shape, in_specs, out_specs=VMEM, scratch_shapes=(), limit=4, cost=None, aliases=None):
    return pl.pallas_call(
        kernel,
        in_specs=in_specs,
        out_specs=out_specs,
        out_shape=out_shape,
        scratch_shapes=scratch_shapes,
        cost_estimate=cost,
        input_output_aliases=aliases or {},
        compiler_params=pltpu.CompilerParams(vmem_limit_bytes=limit * 2**20),
        name=name,
    )


def spread(block, axes, count):
    return lax.all_to_all(jnp.broadcast_to(block[None], (count, *block.shape)), axes, 0, 0)


def local(sizes, grad, error, q_in):
    across, along, shards, cores = sizes["x"], sizes["y"], sizes["z"], sizes["core"]
    planes = across * along
    replicas = planes * cores
    grad, error = grad[0], error[0]
    height, width = grad.shape
    cols, rank = q_in.shape
    half = cols // cores
    core, z = lax.axis_index("core"), lax.axis_index("z")
    swap = [(0, 1), (1, 0)]
    array = jax.ShapeDtypeStruct

    pieces = array((along, height, half), BF16)
    staged = pltpu.VMEM((height, width), BF16)

    def merge(which, name, cost):
        return call(
            merge_kernel, name, pieces, [SMEM, HBM, HBM], VMEM,
            [pltpu.VMEM(pieces.shape, BF16)] * 2 + [pltpu.SemaphoreType.DMA((2, along))],
            limit=MOST, cost=cost,
        )(which.reshape(1), grad, error)

    give, keep = merge(1 - core, "give", LIGHT), merge(core, "keep", WEIGHT)
    took = lax.ppermute(give, "core", swap)
    pair = call(pair_kernel, "pair", array((along, half, height), F32), [VMEM, VMEM], limit=12, cost=LIGHT)(keep, took)
    slab = lax.psum_scatter(pair, "y", scatter_dimension=0, tiled=True)[0]

    q_mine = call(
        slots_kernel, "slots", array((shards, rank, half), BF16), [SMEM, HBM], HBM,
        [pltpu.SemaphoreType.DMA((shards,))], limit=FULL,
    )(core.reshape(1), q_in.T)
    q_all = lax.all_to_all(q_mine, "z", 0, 0)
    first, second = ("x", "core"), "y"
    left = call(
        left_kernel, "left", array((across * cores, rank, height), F32), [VMEM] * 3,
        limit=8, cost=WEIGHT,
    )(q_all, keep, took)
    left = lax.all_to_all(left, first, 0, 0)
    left = call(sum_kernel, "sum", array((along, rank, height), F32), [VMEM])(left)
    left = lax.all_to_all(left, second, 0, 0)
    left_sum, gram = call(
        gram_kernel, "gram",
        [array((rank, height), F32), array((shards, rank // 2, 2 * rank), F32)],
        [VMEM], [VMEM, VMEM],
    )(left)
    grams = lax.all_to_all(gram, "z", 0, 0)
    p_factor, p_round = call(
        factor_kernel, "factor",
        [array((rank, height), F32), array((height, rank), BF16)],
        [VMEM, VMEM], [VMEM, VMEM],
    )(grams, left_sum)

    fold = half // across
    slab = lax.all_to_all(slab.reshape(across, fold, height), "x", 0, 0)
    term = call(
        right_kernel, "right", array((shards, fold // 2, 2 * rank), F32), [VMEM, VMEM]
    )(slab, p_round)
    q_mine = (lax.all_to_all(term, "z", 0, 0).sum(0) / replicas).astype(BF16)
    q_own = spread(q_mine, PLANE, planes)
    q_other = lax.ppermute(q_own, "core", swap)


    def decode(which, name, factor, *before):
        out = (rank, cols if before else half)
        return call(
            decode_kernel, name, [array((height, width), BF16), array(out, BF16)],
            [SMEM] + [VMEM] * 4 + ([HBM, VMEM] if before else []), [HBM, HBM],
            [
                pltpu.VMEM(pieces.shape, BF16), pltpu.VMEM(out, BF16),
                pltpu.SemaphoreType.DMA((along + 1,)),
            ],
            limit=12, aliases={5: 0} if before else None,
        )(jnp.stack([which, z]), p_round, factor, grad, error, *before)

    new_error, q_next = decode(1 - core, "other", q_other, *decode(core, "own", q_own))
    return new_error[None], p_factor.T, q_next.T


def solution(mesh):
    sizes = {"x": 4, "y": 8, "core": 2, "z": 8}
    fine = Mesh(mesh.devices.reshape(tuple(sizes.values())), tuple(sizes))
    placed = (P(REPLICA, "z", None), P(REPLICA, "z", None), P("z", None))
    return jax.shard_map(
        functools.partial(local, sizes),
        mesh=fine,
        in_specs=placed,
        out_specs=(P(REPLICA, "z", None), P("z", None), P("z", None)),
        check_vma=False,
    )
```

```python
import functools

import jax
import jax.numpy as jnp
from jax import lax
from jax.experimental import pallas as pl
from jax.experimental.pallas import tpu as pltpu
from jax.sharding import Mesh, PartitionSpec as P

F32, BF16 = jnp.float32, jnp.bfloat16
SMEM = pl.BlockSpec(memory_space=pltpu.SMEM)
VMEM = pl.BlockSpec(memory_space=pltpu.VMEM)
HBM = pl.BlockSpec(memory_space=pltpu.HBM)
PLANE = ("x", "y")
REPLICA = ("x", "y", "core")
LIGHT = pl.CostEstimate(flops=0, bytes_accessed=0, transcendentals=0)
WEIGHT = pl.CostEstimate(flops=10**11, bytes_accessed=2**21, transcendentals=0)


def merge_kernel(core_ref, grad_hbm, error_hbm, out_ref, grad, error, sems):
    parts, _, half = out_ref.shape
    copies = []
    for i in range(parts):
        at = pl.ds(pl.multiple_of((2 * i + core_ref[0]) * half, half), half)
        copies.append(
            [
                pltpu.make_async_copy(src.at[:, at], dst.at[i], sems.at[j, i])
                for j, (src, dst) in enumerate(((grad_hbm, grad), (error_hbm, error)))
            ]
        )
        for copy in copies[-1]:
            copy.start()
    for i in range(parts):
        for copy in copies[i]:
            copy.wait()
        out_ref[i] = (grad[i].astype(F32) + error[i].astype(F32)).astype(BF16)


def pair_kernel(keep_ref, took_ref, out_ref):
    for i in range(out_ref.shape[0]):
        out_ref[i] = (keep_ref[i].astype(F32) + took_ref[i].astype(F32)).T


def slots_kernel(core_ref, factor_hbm, out_hbm, mine, sems):
    many, _, half = out_hbm.shape
    at = pl.ds(pl.multiple_of(core_ref[0] * half, half), half)
    read = pltpu.make_async_copy(factor_hbm.at[:, at], mine, sems.at[many])
    read.start()
    read.wait()
    copies = [
        pltpu.make_async_copy(mine, out_hbm.at[i], sems.at[i]) for i in range(many)
    ]
    for copy in copies:
        copy.start()
    for copy in copies:
        copy.wait()


def left_kernel(factor_ref, keep_ref, took_ref, out_ref):
    height = keep_ref.shape[1]
    total = None
    for i in range(keep_ref.shape[0]):
        both = jnp.concatenate([keep_ref[i], took_ref[i]], axis=0)
        term = lax.dot_general(
            factor_ref[i], both, (((1,), (1,)), ((), ())), preferred_element_type=F32
        )
        total = term if total is None else total + term
    out_ref[...] = total[:, :height] + total[:, height:]


def gram_kernel(left_ref, out_ref):
    left = left_ref[...]
    gram = lax.dot_general(
        left, left, (((1,), (1,)), ((), ())),
        precision=lax.Precision.HIGHEST, preferred_element_type=F32,
    )
    packed = jnp.concatenate(jnp.split(gram, 2, axis=0), axis=1)
    for i in range(out_ref.shape[0]):
        out_ref[i] = packed


def factor_kernel(grams_ref, left_ref, factor_ref, round_ref):
    packed = grams_ref[0]
    for part in range(1, grams_ref.shape[0]):
        packed = packed + grams_ref[part]
    rank = packed.shape[1] // 2
    gram = jnp.concatenate([packed[:, :rank], packed[:, rank:]], axis=0)
    gram = jnp.concatenate([gram, gram], axis=1)
    blocks = rank // 8
    g = [gram[8 * n : 8 * n + 8] for n in range(blocks)]
    p = [left_ref[8 * n : 8 * n + 8, :] for n in range(blocks)]
    full = (8, 2 * rank)
    sub = lax.broadcasted_iota(jnp.int32, full, 0)

    def lane(v, k):
        return jnp.broadcast_to(v[:, k : k + 1], full)

    def row(v, k):
        return jnp.broadcast_to(v[k : k + 1, :], full)

    hold = None
    for k in range(0, rank, 4):
        own, at = k // 8, k % 8
        gs = [row(g[own], at + j) for j in range(4)]
        ps = [row(p[own], at + j) for j in range(4)]
        e = {(i, j): lane(gs[i], k + j) for i in range(4) for j in range(i, 4)}
        a, b, d = e[0, 0], e[0, 1], e[1, 1]
        det = a * d - b * b
        inverse = 1.0 / det
        ai, bi, di = a * inverse, b * inverse, d * inverse
        t00, t01 = di * e[0, 2] - bi * e[1, 2], di * e[0, 3] - bi * e[1, 3]
        t10, t11 = ai * e[1, 2] - bi * e[0, 2], ai * e[1, 3] - bi * e[0, 3]
        a2 = e[2, 2] - e[0, 2] * t00 - e[1, 2] * t10
        b2 = e[2, 3] - e[0, 2] * t01 - e[1, 2] * t11
        d2 = e[3, 3] - e[0, 3] * t01 - e[1, 3] * t11
        det2 = a2 * d2 - b2 * b2
        inverse2 = 1.0 / det2
        ai2, bi2, di2 = a2 * inverse2, b2 * inverse2, d2 * inverse2

        def solve(r):
            s2 = r[2] - t00 * r[0] - t10 * r[1]
            s3 = r[3] - t01 * r[0] - t11 * r[1]
            w2, w3 = di2 * s2 - bi2 * s3, ai2 * s3 - bi2 * s2
            q0, q1 = di * r[0] - bi * r[1], ai * r[1] - bi * r[0]
            w0, w1 = q0 - t00 * w2 - t01 * w3, q1 - t10 * w2 - t11 * w3
            return (w0, w1, w2, w3), s2, s3

        u, _, _ = solve(gs)
        v, s2, s3 = solve(ps)
        done = (
            ps[0] / jnp.sqrt(a),
            (ps[1] - (b / a) * ps[0]) / jnp.sqrt(det / a),
            s2 / jnp.sqrt(a2),
            (s3 - (b2 / a2) * s2) / jnp.sqrt(det2 / a2),
        )
        out = done[0]
        for j in range(1, 4):
            out = jnp.where(sub == at + j, done[j], out)
        if at == 0:
            hold = out
        else:
            factor_ref[8 * own : 8 * own + 8, :] = jnp.where(sub < 4, hold, out)
        for n in range(own if at == 0 else own + 1, blocks):
            c = [lane(g[n], k + j) for j in range(4)]
            if n == own:
                c = [jnp.where(sub > at + 3, x, 0.0) for x in c]
            g[n] = g[n] - (c[0] * u[0] + c[1] * u[1]) - (c[2] * u[2] + c[3] * u[3])
            p[n] = p[n] - (c[0] * v[0] + c[1] * v[1]) - (c[2] * v[2] + c[3] * v[3])
    round_ref[...] = factor_ref[...].T.astype(BF16)


def right_kernel(slab_ref, round_ref, out_ref):
    slab = slab_ref[0]
    for i in range(1, slab_ref.shape[0]):
        slab = slab + slab_ref[i]
    term = jnp.dot(
        slab, round_ref[...].astype(F32),
        precision=lax.Precision.HIGHEST, preferred_element_type=F32,
    )
    packed = jnp.concatenate(jnp.split(term, 2, axis=0), axis=1)
    for i in range(out_ref.shape[0]):
        out_ref[i] = packed


def decode_kernel(first, place_ref, round_ref, factor_ref, grad, error, *rest):
    if first:
        out_hbm, next_ref, rounded_ref, out, sems = rest
    else:
        _, half_ref, out_hbm, next_hbm, next_ref, out, sems = rest
        rounded_ref = round_ref
    planes, fold, lanes = factor_ref.shape
    rank, half = lanes // 2, out.shape[-1]
    inner = half // (2 * fold)
    parts = planes // inner
    which = place_ref[0]
    if first:
        fetch = pltpu.make_async_copy(round_ref, rounded_ref, sems.at[parts])
        fetch.start()

    def factor(part):
        pieces = []
        for x in range(inner):
            piece = factor_ref[x * parts + part]
            pieces += [piece[:, :rank], piece[:, rank:]]
        return jnp.concatenate(pieces, axis=0)

    mine = factor(place_ref[1]).astype(F32).T.astype(BF16)
    sent = []
    if first:
        next_ref[...] = mine
        fetch.wait()
    else:
        for at, part in ((which, mine), (1 - which, half_ref[...])):
            next_ref[:, pl.ds(pl.multiple_of(at * half, half), half)] = part
        sent.append(pltpu.make_async_copy(next_ref, next_hbm, sems.at[parts]))
        sent[-1].start()
    rounded = rounded_ref[...]
    for i in range(parts):
        decoded = lax.dot_general(
            rounded, factor(i), (((1,), (1,)), ((), ())), preferred_element_type=F32
        )
        at = pl.ds(pl.multiple_of((2 * i + which) * half, half), half)
        out[i] = (
            grad[:, at].astype(F32) + error[:, at].astype(F32) - decoded
        ).astype(BF16)
        sent.append(pltpu.make_async_copy(out.at[i], out_hbm.at[:, at], sems.at[i]))
        sent[-1].start()
    for copy in sent:
        copy.wait()


def call(kernel, name, out_shape, in_specs, out_specs=VMEM, scratch_shapes=(), limit=4, cost=None, aliases=None):
    return pl.pallas_call(
        kernel,
        in_specs=in_specs,
        out_specs=out_specs,
        out_shape=out_shape,
        scratch_shapes=scratch_shapes,
        cost_estimate=cost,
        input_output_aliases=aliases or {},
        compiler_params=pltpu.CompilerParams(vmem_limit_bytes=limit * 2**20),
        name=name,
    )


def in_hbm(x):
    return pltpu.with_memory_space_constraint(x, pltpu.HBM)


def spread(block, axes, count):
    return lax.all_to_all(jnp.broadcast_to(block[None], (count, *block.shape)), axes, 0, 0)


def local(sizes, grad, error, q_in):
    across, along, shards, cores = sizes["x"], sizes["y"], sizes["z"], sizes["core"]
    planes = across * along
    replicas = planes * cores
    grad, error = grad[0], error[0]
    height, width = grad.shape
    cols, rank = q_in.shape
    half = cols // cores
    core, z = lax.axis_index("core"), lax.axis_index("z")
    swap = [(0, 1), (1, 0)]
    array = jax.ShapeDtypeStruct

    pieces = array((along, height, half), BF16)

    def merge(which, name, cost):
        return call(
            merge_kernel, name, pieces, [SMEM, HBM, HBM], VMEM,
            [pltpu.VMEM(pieces.shape, BF16)] * 2 + [pltpu.SemaphoreType.DMA((2, along))],
            limit=12, cost=cost,
        )(which.reshape(1), in_hbm(grad), in_hbm(error))

    give, keep = merge(1 - core, "give", LIGHT), merge(core, "keep", WEIGHT)
    took = lax.ppermute(give, "core", swap)
    pair = call(pair_kernel, "pair", array((along, half, height), F32), [VMEM, VMEM], limit=12, cost=LIGHT)(keep, took)
    slab = lax.psum_scatter(pair, "y", scatter_dimension=0, tiled=True)[0]

    q_mine = call(
        slots_kernel, "slots", array((shards, rank, half), BF16), [SMEM, HBM], HBM,
        [pltpu.VMEM((rank, half), BF16), pltpu.SemaphoreType.DMA((shards + 1,))],
    )(core.reshape(1), in_hbm(q_in.T))
    q_all = lax.all_to_all(q_mine, "z", 0, 0)
    left = call(left_kernel, "left", array((rank, height), F32), [VMEM] * 3, limit=8, cost=WEIGHT)(
        q_all, keep, took
    )
    left_row = lax.all_to_all(left.reshape(replicas, -1, height), REPLICA, 0, 0).sum(0)
    left_sum = spread(left_row, REPLICA, replicas).reshape(rank, height)

    gram = call(gram_kernel, "gram", array((shards, rank // 2, 2 * rank), F32), [VMEM])(
        left_sum
    )
    grams = lax.all_to_all(gram, "z", 0, 0)
    p_factor, p_round = call(
        factor_kernel, "factor",
        [array((rank, height), F32), array((height, rank), BF16)],
        [VMEM, VMEM], [VMEM, VMEM],
    )(grams, left_sum)

    fold = half // across
    slab = lax.all_to_all(slab.reshape(across, fold, height), "x", 0, 0)
    term = call(
        right_kernel, "right", array((shards, fold // 2, 2 * rank), F32), [VMEM, VMEM]
    )(slab, p_round)
    q_mine = (lax.all_to_all(term, "z", 0, 0).sum(0) / replicas).astype(BF16)
    q_own = spread(q_mine, PLANE, planes)
    q_other = lax.ppermute(q_own, "core", swap)


    errors, halves = array((height, width), BF16), array((rank, half), BF16)
    staged = [pltpu.VMEM(pieces.shape, BF16), pltpu.SemaphoreType.DMA((along + 1,))]
    new_error, q_half, rounded = call(
        functools.partial(decode_kernel, True), "own", [errors, halves, p_round],
        [SMEM, HBM] + [VMEM] * 3, [HBM, VMEM, VMEM], staged, limit=12,
    )(jnp.stack([core, z]), in_hbm(p_round), q_own, grad, error)
    new_error, q_next = call(
        functools.partial(decode_kernel, False), "other",
        [errors, array((rank, cols), BF16)],
        [SMEM] + [VMEM] * 4 + [HBM, VMEM], [HBM, HBM],
        [pltpu.VMEM((rank, cols), BF16)] + staged, limit=12, aliases={5: 0},
    )(jnp.stack([1 - core, z]), rounded, q_other, grad, error, new_error, q_half)
    return new_error[None], p_factor.T, q_next.T


def solution(mesh):
    sizes = {"x": 4, "y": 8, "core": 2, "z": 8}
    fine = Mesh(mesh.devices.reshape(tuple(sizes.values())), tuple(sizes))
    placed = (P(REPLICA, "z", None), P(REPLICA, "z", None), P("z", None))
    return jax.shard_map(
        functools.partial(local, sizes),
        mesh=fine,
        in_specs=placed,
        out_specs=(P(REPLICA, "z", None), P("z", None), P("z", None)),
        check_vma=False,
    )
```

```python
import functools

import jax
import jax.numpy as jnp
from jax import lax
from jax.experimental import pallas as pl
from jax.experimental.pallas import tpu as pltpu
from jax.sharding import Mesh, PartitionSpec as P

F32, BF16 = jnp.float32, jnp.bfloat16
SMEM = pl.BlockSpec(memory_space=pltpu.SMEM)
VMEM = pl.BlockSpec(memory_space=pltpu.VMEM)
HBM = pl.BlockSpec(memory_space=pltpu.HBM)
PLANE = ("x", "y")
REPLICA = ("x", "y", "core")
LIGHT = pl.CostEstimate(flops=0, bytes_accessed=0, transcendentals=0)
WEIGHT = pl.CostEstimate(flops=10**11, bytes_accessed=2**21, transcendentals=0)


def fetch_half(which, many, half, sources, places, sems):
    copies = []
    for i in range(many):
        at = pl.ds(pl.multiple_of((2 * i + which) * half, half), half)
        copies.append(
            [
                pltpu.make_async_copy(source.at[:, at], place.at[i], sems.at[j, i])
                for j, (source, place) in enumerate(zip(sources, places))
            ]
        )
        for copy in copies[-1]:
            copy.start()
    return copies


def merge(copies, grad, error, out_ref):
    for i, pair in enumerate(copies):
        for copy in pair:
            copy.wait()
        out_ref[i] = (grad[i].astype(F32) + error[i].astype(F32)).astype(BF16)


def open_kernel(core_ref, factor_hbm, grad_hbm, error_hbm, slots_hbm, give_ref, mine, grad, error, sems):
    many, _, half = give_ref.shape
    core = core_ref[0]
    at = pl.ds(pl.multiple_of(core * half, half), half)
    read = pltpu.make_async_copy(factor_hbm.at[:, at], mine, sems.at[2, 0])
    read.start()
    copies = fetch_half(1 - core, many, half, (grad_hbm, error_hbm), (grad, error), sems)
    read.wait()
    slots = [
        pltpu.make_async_copy(mine, slots_hbm.at[i], sems.at[3, i]) for i in range(many)
    ]
    for copy in slots:
        copy.start()
    merge(copies, grad, error, give_ref)
    for copy in slots:
        copy.wait()


def keep_kernel(core_ref, grad_hbm, error_hbm, keep_ref, grad, error, sems):
    many, _, half = keep_ref.shape
    sources, places = (grad_hbm, error_hbm), (grad, error)
    copies = fetch_half(core_ref[0], many, half, sources, places, sems)
    merge(copies, grad, error, keep_ref)


def pair_kernel(keep_ref, took_ref, out_ref):
    for i in range(out_ref.shape[0]):
        out_ref[i] = (keep_ref[i].astype(F32) + took_ref[i].astype(F32)).T


def left_kernel(factor_ref, keep_ref, took_ref, out_ref):
    height = keep_ref.shape[1]
    total = None
    for i in range(keep_ref.shape[0]):
        both = jnp.concatenate([keep_ref[i], took_ref[i]], axis=0)
        term = lax.dot_general(
            factor_ref[i], both, (((1,), (1,)), ((), ())), preferred_element_type=F32
        )
        total = term if total is None else total + term
    out_ref[...] = total[:, :height] + total[:, height:]


def gram_kernel(left_ref, out_ref):
    left = left_ref[...]
    gram = lax.dot_general(
        left, left, (((1,), (1,)), ((), ())),
        precision=lax.Precision.HIGHEST, preferred_element_type=F32,
    )
    packed = jnp.concatenate(jnp.split(gram, 2, axis=0), axis=1)
    for i in range(out_ref.shape[0]):
        out_ref[i] = packed


def factor_kernel(grams_ref, left_ref, factor_ref, round_ref):
    packed = grams_ref[0]
    for part in range(1, grams_ref.shape[0]):
        packed = packed + grams_ref[part]
    rank = packed.shape[1] // 2
    gram = jnp.concatenate([packed[:, :rank], packed[:, rank:]], axis=0)
    gram = jnp.concatenate([gram, gram], axis=1)
    blocks = rank // 8
    g = [gram[8 * n : 8 * n + 8] for n in range(blocks)]
    p = [left_ref[8 * n : 8 * n + 8, :] for n in range(blocks)]
    full = (8, 2 * rank)
    sub = lax.broadcasted_iota(jnp.int32, full, 0)

    def lane(v, k):
        return jnp.broadcast_to(v[:, k : k + 1], full)

    def row(v, k):
        return jnp.broadcast_to(v[k : k + 1, :], full)

    hold = None
    for k in range(0, rank, 4):
        own, at = k // 8, k % 8
        gs = [row(g[own], at + j) for j in range(4)]
        ps = [row(p[own], at + j) for j in range(4)]
        e = {(i, j): lane(gs[i], k + j) for i in range(4) for j in range(i, 4)}
        a, b, d = e[0, 0], e[0, 1], e[1, 1]
        det = a * d - b * b
        inverse = 1.0 / det
        ai, bi, di = a * inverse, b * inverse, d * inverse
        t00, t01 = di * e[0, 2] - bi * e[1, 2], di * e[0, 3] - bi * e[1, 3]
        t10, t11 = ai * e[1, 2] - bi * e[0, 2], ai * e[1, 3] - bi * e[0, 3]
        a2 = e[2, 2] - e[0, 2] * t00 - e[1, 2] * t10
        b2 = e[2, 3] - e[0, 2] * t01 - e[1, 2] * t11
        d2 = e[3, 3] - e[0, 3] * t01 - e[1, 3] * t11
        det2 = a2 * d2 - b2 * b2
        inverse2 = 1.0 / det2
        ai2, bi2, di2 = a2 * inverse2, b2 * inverse2, d2 * inverse2

        def solve(r):
            s2 = r[2] - t00 * r[0] - t10 * r[1]
            s3 = r[3] - t01 * r[0] - t11 * r[1]
            w2, w3 = di2 * s2 - bi2 * s3, ai2 * s3 - bi2 * s2
            q0, q1 = di * r[0] - bi * r[1], ai * r[1] - bi * r[0]
            w0, w1 = q0 - t00 * w2 - t01 * w3, q1 - t10 * w2 - t11 * w3
            return (w0, w1, w2, w3), s2, s3

        u, _, _ = solve(gs)
        v, s2, s3 = solve(ps)
        done = (
            ps[0] / jnp.sqrt(a),
            (ps[1] - (b / a) * ps[0]) / jnp.sqrt(det / a),
            s2 / jnp.sqrt(a2),
            (s3 - (b2 / a2) * s2) / jnp.sqrt(det2 / a2),
        )
        out = done[0]
        for j in range(1, 4):
            out = jnp.where(sub == at + j, done[j], out)
        if at == 0:
            hold = out
        else:
            factor_ref[8 * own : 8 * own + 8, :] = jnp.where(sub < 4, hold, out)
        for n in range(own if at == 0 else own + 1, blocks):
            c = [lane(g[n], k + j) for j in range(4)]
            if n == own:
                c = [jnp.where(sub > at + 3, x, 0.0) for x in c]
            g[n] = g[n] - (c[0] * u[0] + c[1] * u[1]) - (c[2] * u[2] + c[3] * u[3])
            p[n] = p[n] - (c[0] * v[0] + c[1] * v[1]) - (c[2] * v[2] + c[3] * v[3])
    round_ref[...] = factor_ref[...].T.astype(BF16)


def right_kernel(slab_ref, round_ref, out_ref):
    slab = slab_ref[0]
    for i in range(1, slab_ref.shape[0]):
        slab = slab + slab_ref[i]
    term = jnp.dot(
        slab, round_ref[...].astype(F32),
        precision=lax.Precision.HIGHEST, preferred_element_type=F32,
    )
    packed = jnp.concatenate(jnp.split(term, 2, axis=0), axis=1)
    for i in range(out_ref.shape[0]):
        out_ref[i] = packed


def decode_kernel(first, place_ref, round_ref, factor_ref, grad, error, *rest):
    if first:
        out_hbm, next_ref, rounded_ref, out, sems = rest
    else:
        _, half_ref, out_hbm, next_hbm, next_ref, out, sems = rest
        rounded_ref = round_ref
    planes, fold, lanes = factor_ref.shape
    rank, half = lanes // 2, out.shape[-1]
    inner = half // (2 * fold)
    parts = planes // inner
    which = place_ref[0]
    if first:
        fetch = pltpu.make_async_copy(round_ref, rounded_ref, sems.at[parts])
        fetch.start()

    def factor(part):
        pieces = []
        for x in range(inner):
            piece = factor_ref[x * parts + part]
            pieces += [piece[:, :rank], piece[:, rank:]]
        return jnp.concatenate(pieces, axis=0)

    mine = factor(place_ref[1]).astype(F32).T.astype(BF16)
    sent = []
    if first:
        next_ref[...] = mine
        fetch.wait()
    else:
        for at, part in ((which, mine), (1 - which, half_ref[...])):
            next_ref[:, pl.ds(pl.multiple_of(at * half, half), half)] = part
        sent.append(pltpu.make_async_copy(next_ref, next_hbm, sems.at[parts]))
        sent[-1].start()
    rounded = rounded_ref[...]
    for i in range(parts):
        decoded = lax.dot_general(
            rounded, factor(i), (((1,), (1,)), ((), ())), preferred_element_type=F32
        )
        at = pl.ds(pl.multiple_of((2 * i + which) * half, half), half)
        out[i] = (
            grad[:, at].astype(F32) + error[:, at].astype(F32) - decoded
        ).astype(BF16)
        sent.append(pltpu.make_async_copy(out.at[i], out_hbm.at[:, at], sems.at[i]))
        sent[-1].start()
    for copy in sent:
        copy.wait()


def call(kernel, name, out_shape, in_specs, out_specs=VMEM, scratch_shapes=(), limit=4, cost=None, aliases=None):
    return pl.pallas_call(
        kernel,
        in_specs=in_specs,
        out_specs=out_specs,
        out_shape=out_shape,
        scratch_shapes=scratch_shapes,
        cost_estimate=cost,
        input_output_aliases=aliases or {},
        compiler_params=pltpu.CompilerParams(vmem_limit_bytes=limit * 2**20),
        name=name,
    )


def in_hbm(x):
    return pltpu.with_memory_space_constraint(x, pltpu.HBM)


def spread(block, axes, count):
    return lax.all_to_all(jnp.broadcast_to(block[None], (count, *block.shape)), axes, 0, 0)


def local(sizes, grad, error, q_in):
    across, along, shards, cores = sizes["x"], sizes["y"], sizes["z"], sizes["core"]
    planes = across * along
    replicas = planes * cores
    grad, error = grad[0], error[0]
    height, width = grad.shape
    cols, rank = q_in.shape
    half = cols // cores
    core, z = lax.axis_index("core"), lax.axis_index("z")
    swap = [(0, 1), (1, 0)]
    array = jax.ShapeDtypeStruct

    pieces = array((along, height, half), BF16)

    own_core = core.reshape(1)
    held = [pltpu.VMEM(pieces.shape, BF16)] * 2
    slots, give = call(
        open_kernel, "open", [array((shards, rank, half), BF16), pieces],
        [SMEM, HBM, HBM, HBM], [HBM, VMEM],
        [pltpu.VMEM((rank, half), BF16)] + held + [pltpu.SemaphoreType.DMA((4, along))],
        limit=12, cost=LIGHT,
    )(own_core, in_hbm(q_in.T), in_hbm(grad), in_hbm(error))
    keep = call(
        keep_kernel, "keep", pieces, [SMEM, HBM, HBM], VMEM,
        held + [pltpu.SemaphoreType.DMA((2, along))], limit=12, cost=WEIGHT,
    )(own_core, in_hbm(grad), in_hbm(error))
    took = lax.ppermute(give, "core", swap)
    pair = call(pair_kernel, "pair", array((along, half, height), F32), [VMEM, VMEM], limit=12, cost=LIGHT)(keep, took)
    slab = lax.psum_scatter(pair, "y", scatter_dimension=0, tiled=True)[0]

    q_all = lax.all_to_all(slots, "z", 0, 0)
    left = call(left_kernel, "left", array((rank, height), F32), [VMEM] * 3, limit=8, cost=WEIGHT)(
        q_all, keep, took
    )
    left_row = lax.all_to_all(left.reshape(replicas, -1, height), REPLICA, 0, 0).sum(0)
    left_sum = spread(left_row, REPLICA, replicas).reshape(rank, height)

    gram = call(gram_kernel, "gram", array((shards, rank // 2, 2 * rank), F32), [VMEM])(
        left_sum
    )
    grams = lax.all_to_all(gram, "z", 0, 0)
    p_factor, p_round = call(
        factor_kernel, "factor",
        [array((rank, height), F32), array((height, rank), BF16)],
        [VMEM, VMEM], [VMEM, VMEM],
    )(grams, left_sum)

    fold = half // across
    slab = lax.all_to_all(slab.reshape(across, fold, height), "x", 0, 0)
    term = call(
        right_kernel, "right", array((shards, fold // 2, 2 * rank), F32), [VMEM, VMEM]
    )(slab, p_round)
    q_mine = (lax.all_to_all(term, "z", 0, 0).sum(0) / replicas).astype(BF16)
    q_own = spread(q_mine, PLANE, planes)
    q_other = lax.ppermute(q_own, "core", swap)


    errors, halves = array((height, width), BF16), array((rank, half), BF16)
    staged = [pltpu.VMEM(pieces.shape, BF16), pltpu.SemaphoreType.DMA((along + 1,))]
    new_error, q_half, rounded = call(
        functools.partial(decode_kernel, True), "own", [errors, halves, p_round],
        [SMEM, HBM] + [VMEM] * 3, [HBM, VMEM, VMEM], staged, limit=12,
    )(jnp.stack([core, z]), in_hbm(p_round), q_own, grad, error)
    new_error, q_next = call(
        functools.partial(decode_kernel, False), "other",
        [errors, array((rank, cols), BF16)],
        [SMEM] + [VMEM] * 4 + [HBM, VMEM], [HBM, HBM],
        [pltpu.VMEM((rank, cols), BF16)] + staged, limit=12, aliases={5: 0},
    )(jnp.stack([1 - core, z]), rounded, q_other, grad, error, new_error, q_half)
    return new_error[None], p_factor.T, q_next.T


def solution(mesh):
    sizes = {"x": 4, "y": 8, "core": 2, "z": 8}
    fine = Mesh(mesh.devices.reshape(tuple(sizes.values())), tuple(sizes))
    placed = (P(REPLICA, "z", None), P(REPLICA, "z", None), P("z", None))
    return jax.shard_map(
        functools.partial(local, sizes),
        mesh=fine,
        in_specs=placed,
        out_specs=(P(REPLICA, "z", None), P("z", None), P("z", None)),
        check_vma=False,
    )
```

```python
import functools

import jax
import jax.numpy as jnp
from jax import lax
from jax.experimental import pallas as pl
from jax.experimental.pallas import tpu as pltpu
from jax.sharding import Mesh, PartitionSpec as P

F32, BF16 = jnp.float32, jnp.bfloat16
SMEM = pl.BlockSpec(memory_space=pltpu.SMEM)
VMEM = pl.BlockSpec(memory_space=pltpu.VMEM)
HBM = pl.BlockSpec(memory_space=pltpu.HBM)
PLANE = ("x", "y")
REPLICA = ("x", "y", "core")
LIGHT = pl.CostEstimate(flops=0, bytes_accessed=0, transcendentals=0)
WEIGHT = pl.CostEstimate(flops=10**11, bytes_accessed=2**21, transcendentals=0)


def fetch_half(which, many, half, sources, places, sems):
    copies = []
    for i in range(many):
        at = pl.ds(pl.multiple_of((2 * i + which) * half, half), half)
        copies.append(
            [
                pltpu.make_async_copy(source.at[:, at], place.at[i], sems.at[j, i])
                for j, (source, place) in enumerate(zip(sources, places))
            ]
        )
        for copy in copies[-1]:
            copy.start()
    return copies


def merge(copies, grad, error, out_ref):
    for i, pair in enumerate(copies):
        for copy in pair:
            copy.wait()
        out_ref[i] = (grad[i].astype(F32) + error[i].astype(F32)).astype(BF16)


def open_kernel(core_ref, factor_hbm, grad_hbm, error_hbm, slots_hbm, give_ref, mine, grad, error, sems):
    many, _, half = give_ref.shape
    core = core_ref[0]
    at = pl.ds(pl.multiple_of(core * half, half), half)
    read = pltpu.make_async_copy(factor_hbm.at[:, at], mine, sems.at[2, 0])
    read.start()
    copies = fetch_half(1 - core, many, half, (grad_hbm, error_hbm), (grad, error), sems)
    read.wait()
    slots = [
        pltpu.make_async_copy(mine, slots_hbm.at[i], sems.at[3, i]) for i in range(many)
    ]
    for copy in slots:
        copy.start()
    merge(copies, grad, error, give_ref)
    for copy in slots:
        copy.wait()


def keep_kernel(core_ref, grad_hbm, error_hbm, keep_ref, grad, error, sems):
    many, _, half = keep_ref.shape
    sources, places = (grad_hbm, error_hbm), (grad, error)
    copies = fetch_half(core_ref[0], many, half, sources, places, sems)
    merge(copies, grad, error, keep_ref)


def pair_kernel(keep_ref, took_ref, out_ref):
    for i in range(out_ref.shape[0]):
        out_ref[i] = (keep_ref[i].astype(F32) + took_ref[i].astype(F32)).T


def left_kernel(factor_ref, keep_ref, took_ref, out_ref):
    height = keep_ref.shape[1]
    total = None
    for i in range(keep_ref.shape[0]):
        both = jnp.concatenate([keep_ref[i], took_ref[i]], axis=0)
        term = lax.dot_general(
            factor_ref[i], both, (((1,), (1,)), ((), ())), preferred_element_type=F32
        )
        total = term if total is None else total + term
    out_ref[...] = total[:, :height] + total[:, height:]


def gram_kernel(left_ref, out_ref):
    left = left_ref[...]
    gram = lax.dot_general(
        left, left, (((1,), (1,)), ((), ())),
        precision=lax.Precision.HIGHEST, preferred_element_type=F32,
    )
    packed = jnp.concatenate(jnp.split(gram, 2, axis=0), axis=1)
    for i in range(out_ref.shape[0]):
        out_ref[i] = packed


def factor_kernel(grams_ref, left_ref, factor_ref, round_ref):
    packed = grams_ref[0]
    for part in range(1, grams_ref.shape[0]):
        packed = packed + grams_ref[part]
    rank = packed.shape[1] // 2
    gram = jnp.concatenate([packed[:, :rank], packed[:, rank:]], axis=0)
    gram = jnp.concatenate([gram, gram], axis=1)
    blocks = rank // 8
    g = [gram[8 * n : 8 * n + 8] for n in range(blocks)]
    p = [left_ref[8 * n : 8 * n + 8, :] for n in range(blocks)]
    full = (8, 2 * rank)
    sub = lax.broadcasted_iota(jnp.int32, full, 0)

    def lane(v, k):
        return jnp.broadcast_to(v[:, k : k + 1], full)

    def row(v, k):
        return jnp.broadcast_to(v[k : k + 1, :], full)

    hold = None
    for k in range(0, rank, 4):
        own, at = k // 8, k % 8
        gs = [row(g[own], at + j) for j in range(4)]
        ps = [row(p[own], at + j) for j in range(4)]
        e = {(i, j): lane(gs[i], k + j) for i in range(4) for j in range(i, 4)}
        a, b, d = e[0, 0], e[0, 1], e[1, 1]
        det = a * d - b * b
        inverse = 1.0 / det
        ai, bi, di = a * inverse, b * inverse, d * inverse
        t00, t01 = di * e[0, 2] - bi * e[1, 2], di * e[0, 3] - bi * e[1, 3]
        t10, t11 = ai * e[1, 2] - bi * e[0, 2], ai * e[1, 3] - bi * e[0, 3]
        a2 = e[2, 2] - e[0, 2] * t00 - e[1, 2] * t10
        b2 = e[2, 3] - e[0, 2] * t01 - e[1, 2] * t11
        d2 = e[3, 3] - e[0, 3] * t01 - e[1, 3] * t11
        det2 = a2 * d2 - b2 * b2
        inverse2 = 1.0 / det2
        ai2, bi2, di2 = a2 * inverse2, b2 * inverse2, d2 * inverse2

        def solve(r):
            s2 = r[2] - t00 * r[0] - t10 * r[1]
            s3 = r[3] - t01 * r[0] - t11 * r[1]
            w2, w3 = di2 * s2 - bi2 * s3, ai2 * s3 - bi2 * s2
            q0, q1 = di * r[0] - bi * r[1], ai * r[1] - bi * r[0]
            w0, w1 = q0 - t00 * w2 - t01 * w3, q1 - t10 * w2 - t11 * w3
            return (w0, w1, w2, w3), s2, s3

        u, _, _ = solve(gs)
        v, s2, s3 = solve(ps)
        done = (
            ps[0] / jnp.sqrt(a),
            (ps[1] - (b / a) * ps[0]) / jnp.sqrt(det / a),
            s2 / jnp.sqrt(a2),
            (s3 - (b2 / a2) * s2) / jnp.sqrt(det2 / a2),
        )
        out = done[0]
        for j in range(1, 4):
            out = jnp.where(sub == at + j, done[j], out)
        if at == 0:
            hold = out
        else:
            factor_ref[8 * own : 8 * own + 8, :] = jnp.where(sub < 4, hold, out)
        for n in range(own if at == 0 else own + 1, blocks):
            c = [lane(g[n], k + j) for j in range(4)]
            if n == own:
                c = [jnp.where(sub > at + 3, x, 0.0) for x in c]
            g[n] = g[n] - (c[0] * u[0] + c[1] * u[1]) - (c[2] * u[2] + c[3] * u[3])
            p[n] = p[n] - (c[0] * v[0] + c[1] * v[1]) - (c[2] * v[2] + c[3] * v[3])
    round_ref[...] = factor_ref[...].T.astype(BF16)


def right_kernel(slab_ref, round_ref, out_ref):
    slab = slab_ref[0]
    for i in range(1, slab_ref.shape[0]):
        slab = slab + slab_ref[i]
    term = jnp.dot(
        slab, round_ref[...].astype(F32),
        precision=lax.Precision.HIGHEST, preferred_element_type=F32,
    )
    packed = jnp.concatenate(jnp.split(term, 2, axis=0), axis=1)
    for i in range(out_ref.shape[0]):
        out_ref[i] = packed


def decode_kernel(first, place_ref, round_ref, factor_ref, grad, error, *rest):
    if first:
        out, next_ref, rounded_ref, sems = rest
    else:
        early, half_ref, out_hbm, next_hbm, next_ref, out, sems = rest
        rounded_ref = round_ref
    planes, fold, lanes = factor_ref.shape
    rank, half = lanes // 2, out.shape[-1]
    inner = half // (2 * fold)
    parts = planes // inner
    which = place_ref[0]

    def columns(i, core):
        return pl.ds(pl.multiple_of((2 * i + core) * half, half), half)

    sent = []
    if first:
        fetch = pltpu.make_async_copy(round_ref, rounded_ref, sems.at[0])
        fetch.start()
    else:
        for i in range(parts):
            to = out_hbm.at[:, columns(i, 1 - which)]
            sent.append(pltpu.make_async_copy(early.at[i], to, sems.at[parts + 1 + i]))
            sent[-1].start()

    def factor(part):
        pieces = []
        for x in range(inner):
            piece = factor_ref[x * parts + part]
            pieces += [piece[:, :rank], piece[:, rank:]]
        return jnp.concatenate(pieces, axis=0)

    mine = factor(place_ref[1]).astype(F32).T.astype(BF16)
    if first:
        next_ref[...] = mine
        fetch.wait()
    else:
        for at, part in ((which, mine), (1 - which, half_ref[...])):
            next_ref[:, pl.ds(pl.multiple_of(at * half, half), half)] = part
        sent.append(pltpu.make_async_copy(next_ref, next_hbm, sems.at[parts]))
        sent[-1].start()
    rounded = rounded_ref[...]
    for i in range(parts):
        decoded = lax.dot_general(
            rounded, factor(i), (((1,), (1,)), ((), ())), preferred_element_type=F32
        )
        at = columns(i, which)
        out[i] = (
            grad[:, at].astype(F32) + error[:, at].astype(F32) - decoded
        ).astype(BF16)
        if not first:
            sent.append(pltpu.make_async_copy(out.at[i], out_hbm.at[:, at], sems.at[i]))
            sent[-1].start()
    for copy in sent:
        copy.wait()


def call(kernel, name, out_shape, in_specs, out_specs=VMEM, scratch_shapes=(), limit=4, cost=None):
    return pl.pallas_call(
        kernel,
        in_specs=in_specs,
        out_specs=out_specs,
        out_shape=out_shape,
        scratch_shapes=scratch_shapes,
        cost_estimate=cost,
        compiler_params=pltpu.CompilerParams(vmem_limit_bytes=limit * 2**20),
        name=name,
    )


def in_hbm(x):
    return pltpu.with_memory_space_constraint(x, pltpu.HBM)


def spread(block, axes, count):
    return lax.all_to_all(jnp.broadcast_to(block[None], (count, *block.shape)), axes, 0, 0)


def local(sizes, grad, error, q_in):
    across, along, shards, cores = sizes["x"], sizes["y"], sizes["z"], sizes["core"]
    planes = across * along
    replicas = planes * cores
    grad, error = grad[0], error[0]
    height, width = grad.shape
    cols, rank = q_in.shape
    half = cols // cores
    core, z = lax.axis_index("core"), lax.axis_index("z")
    swap = [(0, 1), (1, 0)]
    array = jax.ShapeDtypeStruct

    pieces = array((along, height, half), BF16)

    own_core = core.reshape(1)
    held = [pltpu.VMEM(pieces.shape, BF16)] * 2
    slots, give = call(
        open_kernel, "open", [array((shards, rank, half), BF16), pieces],
        [SMEM, HBM, HBM, HBM], [HBM, VMEM],
        [pltpu.VMEM((rank, half), BF16)] + held + [pltpu.SemaphoreType.DMA((4, along))],
        limit=12, cost=LIGHT,
    )(own_core, in_hbm(q_in.T), in_hbm(grad), in_hbm(error))
    keep = call(
        keep_kernel, "keep", pieces, [SMEM, HBM, HBM], VMEM,
        held + [pltpu.SemaphoreType.DMA((2, along))], limit=12, cost=WEIGHT,
    )(own_core, in_hbm(grad), in_hbm(error))
    took = lax.ppermute(give, "core", swap)
    pair = call(pair_kernel, "pair", array((along, half, height), F32), [VMEM, VMEM], limit=12, cost=LIGHT)(keep, took)
    slab = lax.psum_scatter(pair, "y", scatter_dimension=0, tiled=True)[0]

    q_all = lax.all_to_all(slots, "z", 0, 0)
    left = call(left_kernel, "left", array((rank, height), F32), [VMEM] * 3, limit=8, cost=WEIGHT)(
        q_all, keep, took
    )
    left_row = lax.all_to_all(left.reshape(replicas, -1, height), REPLICA, 0, 0).sum(0)
    left_sum = spread(left_row, REPLICA, replicas).reshape(rank, height)

    gram = call(gram_kernel, "gram", array((shards, rank // 2, 2 * rank), F32), [VMEM])(
        left_sum
    )
    grams = lax.all_to_all(gram, "z", 0, 0)
    p_factor, p_round = call(
        factor_kernel, "factor",
        [array((rank, height), F32), array((height, rank), BF16)],
        [VMEM, VMEM], [VMEM, VMEM],
    )(grams, left_sum)

    fold = half // across
    slab = lax.all_to_all(slab.reshape(across, fold, height), "x", 0, 0)
    term = call(
        right_kernel, "right", array((shards, fold // 2, 2 * rank), F32), [VMEM, VMEM]
    )(slab, p_round)
    q_mine = (lax.all_to_all(term, "z", 0, 0).sum(0) / replicas).astype(BF16)
    q_own = spread(q_mine, PLANE, planes)
    q_other = lax.ppermute(q_own, "core", swap)


    early, q_half, rounded = call(
        functools.partial(decode_kernel, True), "own",
        [pieces, array((rank, half), BF16), p_round],
        [SMEM, HBM] + [VMEM] * 3, [VMEM] * 3, [pltpu.SemaphoreType.DMA((1,))], limit=12,
    )(jnp.stack([core, z]), in_hbm(p_round), q_own, grad, error)
    new_error, q_next = call(
        functools.partial(decode_kernel, False), "other",
        [array((height, width), BF16), array((rank, cols), BF16)],
        [SMEM] + [VMEM] * 6, [HBM, HBM],
        [
            pltpu.VMEM((rank, cols), BF16), pltpu.VMEM(pieces.shape, BF16),
            pltpu.SemaphoreType.DMA((2 * along + 1,)),
        ],
        limit=12,
    )(jnp.stack([1 - core, z]), rounded, q_other, grad, error, early, q_half)
    return new_error[None], p_factor.T, q_next.T


def solution(mesh):
    sizes = {"x": 4, "y": 8, "core": 2, "z": 8}
    fine = Mesh(mesh.devices.reshape(tuple(sizes.values())), tuple(sizes))
    placed = (P(REPLICA, "z", None), P(REPLICA, "z", None), P("z", None))
    return jax.shard_map(
        functools.partial(local, sizes),
        mesh=fine,
        in_specs=placed,
        out_specs=(P(REPLICA, "z", None), P("z", None), P("z", None)),
        check_vma=False,
    )
```

```python
import functools

import jax
import jax.numpy as jnp
from jax import lax
from jax.experimental import pallas as pl
from jax.experimental.pallas import tpu as pltpu
from jax.sharding import Mesh, PartitionSpec as P

F32, BF16 = jnp.float32, jnp.bfloat16
SMEM = pl.BlockSpec(memory_space=pltpu.SMEM)
VMEM = pl.BlockSpec(memory_space=pltpu.VMEM)
HBM = pl.BlockSpec(memory_space=pltpu.HBM)
PLANE = ("x", "y")
REPLICA = ("x", "y", "core")
SPREAD = ("core", "y", "x")
LIGHT = pl.CostEstimate(flops=0, bytes_accessed=0, transcendentals=0)
WEIGHT = pl.CostEstimate(flops=10**11, bytes_accessed=2**21, transcendentals=0)


def fetch_half(which, many, half, sources, places, sems):
    copies = []
    for i in range(many):
        at = pl.ds(pl.multiple_of((2 * i + which) * half, half), half)
        copies.append(
            [
                pltpu.make_async_copy(source.at[:, at], place.at[i], sems.at[j, i])
                for j, (source, place) in enumerate(zip(sources, places))
            ]
        )
        for copy in copies[-1]:
            copy.start()
    return copies


def merge(copies, grad, error, out_ref):
    for i, pair in enumerate(copies):
        for copy in pair:
            copy.wait()
        out_ref[i] = (grad[i].astype(F32) + error[i].astype(F32)).astype(BF16)


def open_kernel(core_ref, factor_hbm, grad_hbm, error_hbm, slots_hbm, give_ref, mine, grad, error, sems):
    many, _, half = give_ref.shape
    core = core_ref[0]
    at = pl.ds(pl.multiple_of(core * half, half), half)
    read = pltpu.make_async_copy(factor_hbm.at[:, at], mine, sems.at[2, 0])
    read.start()
    copies = fetch_half(1 - core, many, half, (grad_hbm, error_hbm), (grad, error), sems)
    read.wait()
    slots = [
        pltpu.make_async_copy(mine, slots_hbm.at[i], sems.at[3, i]) for i in range(many)
    ]
    for copy in slots:
        copy.start()
    merge(copies, grad, error, give_ref)
    for copy in slots:
        copy.wait()


def keep_kernel(core_ref, grad_hbm, error_hbm, keep_ref, grad, error, sems):
    many, _, half = keep_ref.shape
    sources, places = (grad_hbm, error_hbm), (grad, error)
    copies = fetch_half(core_ref[0], many, half, sources, places, sems)
    merge(copies, grad, error, keep_ref)


def pair_kernel(keep_ref, took_ref, out_ref):
    for i in range(out_ref.shape[0]):
        out_ref[i] = (keep_ref[i].astype(F32) + took_ref[i].astype(F32)).T


def left_kernel(factor_ref, keep_ref, took_ref, out_ref):
    height = keep_ref.shape[1]
    total = None
    for i in range(keep_ref.shape[0]):
        both = jnp.concatenate([keep_ref[i], took_ref[i]], axis=0)
        term = lax.dot_general(
            factor_ref[i], both, (((1,), (1,)), ((), ())), preferred_element_type=F32
        )
        total = term if total is None else total + term
    out_ref[...] = total[:, :height] + total[:, height:]


def gram_kernel(left_ref, out_ref):
    left = left_ref[...]
    gram = lax.dot_general(
        left, left, (((1,), (1,)), ((), ())),
        precision=lax.Precision.HIGHEST, preferred_element_type=F32,
    )
    packed = jnp.concatenate(jnp.split(gram, 2, axis=0), axis=1)
    for i in range(out_ref.shape[0]):
        out_ref[i] = packed


def factor_kernel(grams_ref, left_ref, factor_ref, round_ref):
    packed = grams_ref[0]
    for part in range(1, grams_ref.shape[0]):
        packed = packed + grams_ref[part]
    rank = packed.shape[1] // 2
    gram = jnp.concatenate([packed[:, :rank], packed[:, rank:]], axis=0)
    gram = jnp.concatenate([gram, gram], axis=1)
    blocks = rank // 8
    g = [gram[8 * n : 8 * n + 8] for n in range(blocks)]
    p = [left_ref[8 * n : 8 * n + 8, :] for n in range(blocks)]
    full = (8, 2 * rank)
    sub = lax.broadcasted_iota(jnp.int32, full, 0)

    def lane(v, k):
        return jnp.broadcast_to(v[:, k : k + 1], full)

    def row(v, k):
        return jnp.broadcast_to(v[k : k + 1, :], full)

    hold = None
    for k in range(0, rank, 4):
        own, at = k // 8, k % 8
        gs = [row(g[own], at + j) for j in range(4)]
        ps = [row(p[own], at + j) for j in range(4)]
        e = {(i, j): lane(gs[i], k + j) for i in range(4) for j in range(i, 4)}
        a, b, d = e[0, 0], e[0, 1], e[1, 1]
        det = a * d - b * b
        inverse = 1.0 / det
        ai, bi, di = a * inverse, b * inverse, d * inverse
        t00, t01 = di * e[0, 2] - bi * e[1, 2], di * e[0, 3] - bi * e[1, 3]
        t10, t11 = ai * e[1, 2] - bi * e[0, 2], ai * e[1, 3] - bi * e[0, 3]
        a2 = e[2, 2] - e[0, 2] * t00 - e[1, 2] * t10
        b2 = e[2, 3] - e[0, 2] * t01 - e[1, 2] * t11
        d2 = e[3, 3] - e[0, 3] * t01 - e[1, 3] * t11
        det2 = a2 * d2 - b2 * b2
        inverse2 = 1.0 / det2
        ai2, bi2, di2 = a2 * inverse2, b2 * inverse2, d2 * inverse2

        def solve(r):
            s2 = r[2] - t00 * r[0] - t10 * r[1]
            s3 = r[3] - t01 * r[0] - t11 * r[1]
            w2, w3 = di2 * s2 - bi2 * s3, ai2 * s3 - bi2 * s2
            q0, q1 = di * r[0] - bi * r[1], ai * r[1] - bi * r[0]
            w0, w1 = q0 - t00 * w2 - t01 * w3, q1 - t10 * w2 - t11 * w3
            return (w0, w1, w2, w3), s2, s3

        u, _, _ = solve(gs)
        v, s2, s3 = solve(ps)
        done = (
            ps[0] / jnp.sqrt(a),
            (ps[1] - (b / a) * ps[0]) / jnp.sqrt(det / a),
            s2 / jnp.sqrt(a2),
            (s3 - (b2 / a2) * s2) / jnp.sqrt(det2 / a2),
        )
        out = done[0]
        for j in range(1, 4):
            out = jnp.where(sub == at + j, done[j], out)
        if at == 0:
            hold = out
        else:
            factor_ref[8 * own : 8 * own + 8, :] = jnp.where(sub < 4, hold, out)
        for n in range(own if at == 0 else own + 1, blocks):
            c = [lane(g[n], k + j) for j in range(4)]
            if n == own:
                c = [jnp.where(sub > at + 3, x, 0.0) for x in c]
            g[n] = g[n] - (c[0] * u[0] + c[1] * u[1]) - (c[2] * u[2] + c[3] * u[3])
            p[n] = p[n] - (c[0] * v[0] + c[1] * v[1]) - (c[2] * v[2] + c[3] * v[3])
    round_ref[...] = factor_ref[...].T.astype(BF16)


def right_kernel(slab_ref, round_ref, out_ref):
    slab = slab_ref[0]
    for i in range(1, slab_ref.shape[0]):
        slab = slab + slab_ref[i]
    term = jnp.dot(
        slab, round_ref[...].astype(F32),
        precision=lax.Precision.HIGHEST, preferred_element_type=F32,
    )
    packed = jnp.concatenate(jnp.split(term, 2, axis=0), axis=1)
    for i in range(out_ref.shape[0]):
        out_ref[i] = packed


def decode_kernel(first, core_ref, z_ref, round_ref, factor_ref, grad, error, *rest):
    if first:
        out, next_ref, rounded_ref, sems = rest
    else:
        early, half_ref, out_hbm, next_hbm, next_ref, out, sems = rest
        rounded_ref = round_ref
    planes, fold, lanes = factor_ref.shape
    rank, half = lanes // 2, out.shape[-1]
    inner = half // (2 * fold)
    parts = planes // inner
    which = core_ref[0] if first else 1 - core_ref[0]

    def columns(i, core):
        return pl.ds(pl.multiple_of((2 * i + core) * half, half), half)

    sent = []
    if first:
        fetch = pltpu.make_async_copy(round_ref, rounded_ref, sems.at[0])
        fetch.start()
    else:
        for i in range(parts):
            to = out_hbm.at[:, columns(i, 1 - which)]
            sent.append(pltpu.make_async_copy(early.at[i], to, sems.at[parts + 1 + i]))
            sent[-1].start()

    def factor(part):
        pieces = []
        for x in range(inner):
            piece = factor_ref[x * parts + part]
            pieces += [piece[:, :rank], piece[:, rank:]]
        return jnp.concatenate(pieces, axis=0)

    mine = factor(z_ref[0]).astype(F32).T.astype(BF16)
    if first:
        next_ref[...] = mine
        fetch.wait()
    else:
        for at, part in ((which, mine), (1 - which, half_ref[...])):
            next_ref[:, pl.ds(pl.multiple_of(at * half, half), half)] = part
        sent.append(pltpu.make_async_copy(next_ref, next_hbm, sems.at[parts]))
        sent[-1].start()
    rounded = rounded_ref[...]
    for i in range(parts):
        decoded = lax.dot_general(
            rounded, factor(i), (((1,), (1,)), ((), ())), preferred_element_type=F32
        )
        at = columns(i, which)
        out[i] = (
            grad[:, at].astype(F32) + error[:, at].astype(F32) - decoded
        ).astype(BF16)
        if not first:
            sent.append(pltpu.make_async_copy(out.at[i], out_hbm.at[:, at], sems.at[i]))
            sent[-1].start()
    for copy in sent:
        copy.wait()


def call(kernel, name, out_shape, in_specs, out_specs=VMEM, scratch_shapes=(), limit=4, cost=None):
    return pl.pallas_call(
        kernel,
        in_specs=in_specs,
        out_specs=out_specs,
        out_shape=out_shape,
        scratch_shapes=scratch_shapes,
        cost_estimate=cost,
        compiler_params=pltpu.CompilerParams(vmem_limit_bytes=limit * 2**20),
        name=name,
    )


def in_hbm(x):
    return pltpu.with_memory_space_constraint(x, pltpu.HBM)


def spread(block, axes, count):
    return lax.all_to_all(jnp.broadcast_to(block[None], (count, *block.shape)), axes, 0, 0)


def local(sizes, grad, error, q_in):
    across, along, shards, cores = sizes["x"], sizes["y"], sizes["z"], sizes["core"]
    planes = across * along
    replicas = planes * cores
    grad, error = grad[0], error[0]
    height, width = grad.shape
    cols, rank = q_in.shape
    half = cols // cores
    core, z = lax.axis_index("core"), lax.axis_index("z")
    swap = [(0, 1), (1, 0)]
    array = jax.ShapeDtypeStruct

    pieces = array((along, height, half), BF16)

    own_core = core.reshape(1)
    held = [pltpu.VMEM(pieces.shape, BF16)] * 2
    slots, give = call(
        open_kernel, "open", [array((shards, rank, half), BF16), pieces],
        [SMEM, HBM, HBM, HBM], [HBM, VMEM],
        [pltpu.VMEM((rank, half), BF16)] + held + [pltpu.SemaphoreType.DMA((4, along))],
        limit=12, cost=LIGHT,
    )(own_core, in_hbm(q_in.T), in_hbm(grad), in_hbm(error))
    keep = call(
        keep_kernel, "keep", pieces, [SMEM, HBM, HBM], VMEM,
        held + [pltpu.SemaphoreType.DMA((2, along))], limit=12, cost=WEIGHT,
    )(own_core, in_hbm(grad), in_hbm(error))
    took = lax.ppermute(give, "core", swap)
    pair = call(pair_kernel, "pair", array((along, half, height), F32), [VMEM, VMEM], limit=12, cost=LIGHT)(keep, took)
    slab = lax.psum_scatter(pair, "y", scatter_dimension=0, tiled=True)[0]

    q_all = lax.all_to_all(slots, "z", 0, 0)
    left = call(left_kernel, "left", array((rank, height), F32), [VMEM] * 3, limit=8, cost=WEIGHT)(
        q_all, keep, took
    )
    left_row = lax.all_to_all(left.reshape(replicas, -1, height), SPREAD, 0, 0).sum(0)
    left_sum = spread(left_row, SPREAD, replicas).reshape(rank, height)

    gram = call(gram_kernel, "gram", array((shards, rank // 2, 2 * rank), F32), [VMEM])(
        left_sum
    )
    grams = lax.all_to_all(gram, "z", 0, 0)
    p_factor, p_round = call(
        factor_kernel, "factor",
        [array((rank, height), F32), array((height, rank), BF16)],
        [VMEM, VMEM], [VMEM, VMEM],
    )(grams, left_sum)

    fold = half // across
    slab = lax.all_to_all(slab.reshape(across, fold, height), "x", 0, 0)
    term = call(
        right_kernel, "right", array((shards, fold // 2, 2 * rank), F32), [VMEM, VMEM]
    )(slab, p_round)
    q_mine = (lax.all_to_all(term, "z", 0, 0).sum(0) / replicas).astype(BF16)
    q_own = spread(q_mine, PLANE, planes)
    q_other = lax.ppermute(q_own, "core", swap)


    early, q_half, rounded = call(
        functools.partial(decode_kernel, True), "own",
        [pieces, array((rank, half), BF16), p_round],
        [SMEM, SMEM, HBM] + [VMEM] * 3, [VMEM] * 3, [pltpu.SemaphoreType.DMA((1,))], limit=12,
    )(own_core, z.reshape(1), in_hbm(p_round), q_own, grad, error)
    new_error, q_next = call(
        functools.partial(decode_kernel, False), "other",
        [array((height, width), BF16), array((rank, cols), BF16)],
        [SMEM, SMEM] + [VMEM] * 6, [HBM, HBM],
        [
            pltpu.VMEM((rank, cols), BF16), pltpu.VMEM(pieces.shape, BF16),
            pltpu.SemaphoreType.DMA((2 * along + 1,)),
        ],
        limit=12,
    )(own_core, z.reshape(1), rounded, q_other, grad, error, early, q_half)
    return new_error[None], p_factor.T, q_next.T


def solution(mesh):
    sizes = {"x": 4, "y": 8, "core": 2, "z": 8}
    fine = Mesh(mesh.devices.reshape(tuple(sizes.values())), tuple(sizes))
    placed = (P(REPLICA, "z", None), P(REPLICA, "z", None), P("z", None))
    return jax.shard_map(
        functools.partial(local, sizes),
        mesh=fine,
        in_specs=placed,
        out_specs=(P(REPLICA, "z", None), P("z", None), P("z", None)),
        check_vma=False,
    )
```

```python
import functools

import jax
import jax.numpy as jnp
from jax import lax
from jax.experimental import pallas as pl
from jax.experimental.pallas import tpu as pltpu
from jax.sharding import Mesh, PartitionSpec as P

F32, BF16 = jnp.float32, jnp.bfloat16
SMEM = pl.BlockSpec(memory_space=pltpu.SMEM)
VMEM = pl.BlockSpec(memory_space=pltpu.VMEM)
HBM = pl.BlockSpec(memory_space=pltpu.HBM)
PLANE = ("x", "y")
REPLICA = ("x", "y", "core")
LIGHT = pl.CostEstimate(flops=0, bytes_accessed=0, transcendentals=0)
WEIGHT = pl.CostEstimate(flops=10**11, bytes_accessed=2**21, transcendentals=0)


def fetch_half(which, many, half, sources, places, sems):
    copies = []
    for i in range(many):
        at = pl.ds(pl.multiple_of((2 * i + which) * half, half), half)
        copies.append(
            [
                pltpu.make_async_copy(source.at[:, at], place.at[i], sems.at[j, i])
                for j, (source, place) in enumerate(zip(sources, places))
            ]
        )
        for copy in copies[-1]:
            copy.start()
    return copies


def merge(copies, grad, error, out_ref):
    for i, pair in enumerate(copies):
        for copy in pair:
            copy.wait()
        out_ref[i] = (grad[i].astype(F32) + error[i].astype(F32)).astype(BF16)


def open_kernel(core_ref, factor_hbm, grad_hbm, error_hbm, slots_hbm, give_ref, mine, grad, error, sems):
    many, _, half = give_ref.shape
    core = core_ref[0]
    at = pl.ds(pl.multiple_of(core * half, half), half)
    read = pltpu.make_async_copy(factor_hbm.at[:, at], mine, sems.at[2, 0])
    read.start()
    copies = fetch_half(1 - core, many, half, (grad_hbm, error_hbm), (grad, error), sems)
    read.wait()
    slots = [
        pltpu.make_async_copy(mine, slots_hbm.at[i], sems.at[3, i]) for i in range(many)
    ]
    for copy in slots:
        copy.start()
    merge(copies, grad, error, give_ref)
    for copy in slots:
        copy.wait()


def keep_kernel(core_ref, grad_hbm, error_hbm, keep_ref, grad, error, sems):
    many, _, half = keep_ref.shape
    sources, places = (grad_hbm, error_hbm), (grad, error)
    copies = fetch_half(core_ref[0], many, half, sources, places, sems)
    merge(copies, grad, error, keep_ref)


def pair_kernel(keep_ref, took_ref, out_ref):
    for i in range(out_ref.shape[0]):
        out_ref[i] = (keep_ref[i].astype(F32) + took_ref[i].astype(F32)).T


def left_kernel(factor_ref, keep_ref, took_ref, out_ref):
    height = keep_ref.shape[1]
    total = None
    for i in range(keep_ref.shape[0]):
        both = jnp.concatenate([keep_ref[i], took_ref[i]], axis=0)
        term = lax.dot_general(
            factor_ref[i], both, (((1,), (1,)), ((), ())), preferred_element_type=F32
        )
        total = term if total is None else total + term
    out_ref[...] = total[:, :height] + total[:, height:]


def gram_kernel(left_ref, out_ref):
    left = left_ref[...]
    gram = lax.dot_general(
        left, left, (((1,), (1,)), ((), ())),
        precision=lax.Precision.HIGHEST, preferred_element_type=F32,
    )
    packed = jnp.concatenate(jnp.split(gram, 2, axis=0), axis=1)
    for i in range(out_ref.shape[0]):
        out_ref[i] = packed


def factor_kernel(grams_ref, left_ref, factor_ref, round_ref):
    packed = grams_ref[0]
    for part in range(1, grams_ref.shape[0]):
        packed = packed + grams_ref[part]
    rank = packed.shape[1] // 2
    gram = jnp.concatenate([packed[:, :rank], packed[:, rank:]], axis=0)
    gram = jnp.concatenate([gram, gram], axis=1)
    blocks = rank // 8
    g = [gram[8 * n : 8 * n + 8] for n in range(blocks)]
    p = [left_ref[8 * n : 8 * n + 8, :] for n in range(blocks)]
    full = (8, 2 * rank)
    sub = lax.broadcasted_iota(jnp.int32, full, 0)

    def lane(v, k):
        return jnp.broadcast_to(v[:, k : k + 1], full)

    def row(v, k):
        return jnp.broadcast_to(v[k : k + 1, :], full)

    hold = None
    for k in range(0, rank, 4):
        own, at = k // 8, k % 8
        gs = [row(g[own], at + j) for j in range(4)]
        ps = [row(p[own], at + j) for j in range(4)]
        e = {(i, j): lane(gs[i], k + j) for i in range(4) for j in range(i, 4)}
        a, b, d = e[0, 0], e[0, 1], e[1, 1]
        det = a * d - b * b
        inverse = 1.0 / det
        ai, bi, di = a * inverse, b * inverse, d * inverse
        t00, t01 = di * e[0, 2] - bi * e[1, 2], di * e[0, 3] - bi * e[1, 3]
        t10, t11 = ai * e[1, 2] - bi * e[0, 2], ai * e[1, 3] - bi * e[0, 3]
        a2 = e[2, 2] - e[0, 2] * t00 - e[1, 2] * t10
        b2 = e[2, 3] - e[0, 2] * t01 - e[1, 2] * t11
        d2 = e[3, 3] - e[0, 3] * t01 - e[1, 3] * t11
        det2 = a2 * d2 - b2 * b2
        inverse2 = 1.0 / det2
        ai2, bi2, di2 = a2 * inverse2, b2 * inverse2, d2 * inverse2

        def solve(r):
            s2 = r[2] - t00 * r[0] - t10 * r[1]
            s3 = r[3] - t01 * r[0] - t11 * r[1]
            w2, w3 = di2 * s2 - bi2 * s3, ai2 * s3 - bi2 * s2
            q0, q1 = di * r[0] - bi * r[1], ai * r[1] - bi * r[0]
            w0, w1 = q0 - t00 * w2 - t01 * w3, q1 - t10 * w2 - t11 * w3
            return (w0, w1, w2, w3), s2, s3

        u, _, _ = solve(gs)
        v, s2, s3 = solve(ps)
        done = (
            ps[0] / jnp.sqrt(a),
            (ps[1] - (b / a) * ps[0]) / jnp.sqrt(det / a),
            s2 / jnp.sqrt(a2),
            (s3 - (b2 / a2) * s2) / jnp.sqrt(det2 / a2),
        )
        out = done[0]
        for j in range(1, 4):
            out = jnp.where(sub == at + j, done[j], out)
        if at == 0:
            hold = out
        else:
            factor_ref[8 * own : 8 * own + 8, :] = jnp.where(sub < 4, hold, out)
        for n in range(own if at == 0 else own + 1, blocks):
            c = [lane(g[n], k + j) for j in range(4)]
            if n == own:
                c = [jnp.where(sub > at + 3, x, 0.0) for x in c]
            g[n] = g[n] - (c[0] * u[0] + c[1] * u[1]) - (c[2] * u[2] + c[3] * u[3])
            p[n] = p[n] - (c[0] * v[0] + c[1] * v[1]) - (c[2] * v[2] + c[3] * v[3])
    round_ref[...] = factor_ref[...].T.astype(BF16)


def right_kernel(slab_ref, round_ref, out_ref):
    slab = slab_ref[0]
    for i in range(1, slab_ref.shape[0]):
        slab = slab + slab_ref[i]
    term = jnp.dot(
        slab, round_ref[...].astype(F32),
        precision=lax.Precision.HIGHEST, preferred_element_type=F32,
    )
    packed = jnp.concatenate(jnp.split(term, 2, axis=0), axis=1)
    for i in range(out_ref.shape[0]):
        out_ref[i] = packed


def decode_kernel(first, core_ref, z_ref, round_ref, factor_ref, grad, error, *rest):
    if first:
        out, next_ref, rounded_ref, sems = rest
    else:
        early, half_ref, out_hbm, next_hbm, next_ref, out, sems = rest
        rounded_ref = round_ref
    planes, fold, lanes = factor_ref.shape
    rank, half = lanes // 2, out.shape[-1]
    inner = half // (2 * fold)
    parts = planes // inner
    which = core_ref[0] if first else 1 - core_ref[0]

    def columns(i, core):
        return pl.ds(pl.multiple_of((2 * i + core) * half, half), half)

    sent = []
    if first:
        fetch = pltpu.make_async_copy(round_ref, rounded_ref, sems.at[0])
        fetch.start()
    else:
        for i in range(parts):
            to = out_hbm.at[:, columns(i, 1 - which)]
            sent.append(pltpu.make_async_copy(early.at[i], to, sems.at[parts + 1 + i]))
            sent[-1].start()

    def factor(part):
        pieces = []
        for x in range(inner):
            piece = factor_ref[x * parts + part]
            pieces += [piece[:, :rank], piece[:, rank:]]
        return jnp.concatenate(pieces, axis=0)

    mine = factor(z_ref[0]).astype(F32).T.astype(BF16)
    if first:
        next_ref[...] = mine
        fetch.wait()
    else:
        for at, part in ((which, mine), (1 - which, half_ref[...])):
            next_ref[:, pl.ds(pl.multiple_of(at * half, half), half)] = part
        sent.append(pltpu.make_async_copy(next_ref, next_hbm, sems.at[parts]))
        sent[-1].start()
    rounded = rounded_ref[...]
    for i in range(parts):
        decoded = lax.dot_general(
            rounded, factor(i), (((1,), (1,)), ((), ())), preferred_element_type=F32
        )
        at = columns(i, which)
        out[i] = (
            grad[:, at].astype(F32) + error[:, at].astype(F32) - decoded
        ).astype(BF16)
        if not first:
            sent.append(pltpu.make_async_copy(out.at[i], out_hbm.at[:, at], sems.at[i]))
            sent[-1].start()
    for copy in sent:
        copy.wait()


def call(kernel, name, out_shape, in_specs, out_specs=VMEM, scratch_shapes=(), limit=4, cost=None):
    return pl.pallas_call(
        kernel,
        in_specs=in_specs,
        out_specs=out_specs,
        out_shape=out_shape,
        scratch_shapes=scratch_shapes,
        cost_estimate=cost,
        compiler_params=pltpu.CompilerParams(vmem_limit_bytes=limit * 2**20),
        name=name,
    )


def in_hbm(x):
    return pltpu.with_memory_space_constraint(x, pltpu.HBM)


def spread(block, axes, count):
    return lax.all_to_all(jnp.broadcast_to(block[None], (count, *block.shape)), axes, 0, 0)


def local(sizes, grad, error, q_in):
    across, along, shards, cores = sizes["x"], sizes["y"], sizes["z"], sizes["core"]
    planes = across * along
    replicas = planes * cores
    grad, error = grad[0], error[0]
    height, width = grad.shape
    cols, rank = q_in.shape
    half = cols // cores
    core, z = lax.axis_index("core"), lax.axis_index("z")
    swap = [(0, 1), (1, 0)]
    array = jax.ShapeDtypeStruct

    pieces = array((along, height, half), BF16)

    own_core = core.reshape(1)
    held = [pltpu.VMEM(pieces.shape, BF16)] * 2
    slots, give = call(
        open_kernel, "open", [array((shards, rank, half), BF16), pieces],
        [SMEM, HBM, HBM, HBM], [HBM, VMEM],
        [pltpu.VMEM((rank, half), BF16)] + held + [pltpu.SemaphoreType.DMA((4, along))],
        limit=12, cost=LIGHT,
    )(own_core, in_hbm(q_in.T), in_hbm(grad), in_hbm(error))
    keep = call(
        keep_kernel, "keep", pieces, [SMEM, HBM, HBM], VMEM,
        held + [pltpu.SemaphoreType.DMA((2, along))], limit=12, cost=WEIGHT,
    )(own_core, in_hbm(grad), in_hbm(error))
    took = lax.ppermute(give, "core", swap)
    pair = call(pair_kernel, "pair", array((along, half, height), F32), [VMEM, VMEM], limit=12, cost=LIGHT)(keep, took)
    slab = lax.psum_scatter(pair, "y", scatter_dimension=0, tiled=True)[0]

    q_all = lax.all_to_all(slots, "z", 0, 0)
    left = call(left_kernel, "left", array((rank, height), F32), [VMEM] * 3, limit=8, cost=WEIGHT)(
        q_all, keep, took
    )
    left_row = lax.all_to_all(left.reshape(replicas, -1, height), REPLICA, 0, 0).sum(0)
    left_sum = spread(left_row, REPLICA, replicas).reshape(rank, height)

    gram = call(gram_kernel, "gram", array((shards, rank // 2, 2 * rank), F32), [VMEM])(
        left_sum
    )
    grams = lax.all_to_all(gram, "z", 0, 0)
    p_factor, p_round = call(
        factor_kernel, "factor",
        [array((rank, height), F32), array((height, rank), BF16)],
        [VMEM, VMEM], [VMEM, VMEM],
    )(grams, left_sum)

    fold = half // across
    slab = lax.all_to_all(slab.reshape(across, fold, height), "x", 0, 0)
    term = call(
        right_kernel, "right", array((shards, fold // 2, 2 * rank), F32), [VMEM, VMEM]
    )(slab, p_round)
    q_mine = (lax.all_to_all(term, "z", 0, 0).sum(0) / replicas).astype(BF16)
    q_own = spread(q_mine, PLANE, planes)
    q_other = lax.ppermute(q_own, "core", swap)


    early, q_half, rounded = call(
        functools.partial(decode_kernel, True), "own",
        [pieces, array((rank, half), BF16), p_round],
        [SMEM, SMEM, HBM] + [VMEM] * 3, [VMEM] * 3, [pltpu.SemaphoreType.DMA((1,))], limit=12,
    )(own_core, z.reshape(1), in_hbm(p_round), q_own, grad, error)
    new_error, q_next = call(
        functools.partial(decode_kernel, False), "other",
        [array((height, width), BF16), array((rank, cols), BF16)],
        [SMEM, SMEM] + [VMEM] * 6, [HBM, HBM],
        [
            pltpu.VMEM((rank, cols), BF16), pltpu.VMEM(pieces.shape, BF16),
            pltpu.SemaphoreType.DMA((2 * along + 1,)),
        ],
        limit=12,
    )(own_core, z.reshape(1), rounded, q_other, grad, error, early, q_half)
    return new_error[None], p_factor.T, q_next.T


def solution(mesh):
    sizes = {"x": 4, "y": 8, "core": 2, "z": 8}
    fine = Mesh(mesh.devices.reshape(tuple(sizes.values())), tuple(sizes))
    placed = (P(REPLICA, "z", None), P(REPLICA, "z", None), P("z", None))
    return jax.shard_map(
        functools.partial(local, sizes),
        mesh=fine,
        in_specs=placed,
        out_specs=(P(REPLICA, "z", None), P("z", None), P("z", None)),
        check_vma=False,
    )
```
